128 devices in a mesh: grp: 4 (over x), dp: 32 (over y, z, core).
Axes of the slice: x: 4, y: 4, z: 4, core: 2. Of those that a mesh axis runs over, the one named last changes fastest.
Arguments:
- blocks: bfloat16 [512, 128, 1280], P(('grp', 'dp')), may hold values from -6 to 6
- cotangent: bfloat16 [512, 128, 1280], P(('grp', 'dp')), may hold values from -6 to 6
- modality: int32 [512], P(('grp', 'dp')), may hold values from 0 to 1, as said below
- time_rank: int32 [512], P(('grp', 'dp')), may hold values from 0 to 3, as said below
- qkv_weight: bfloat16 [2, 1280, 1920], P(None, 'dp'), may hold values from -5 to 5
- out_weight: bfloat16 [2, 640, 1280], P(None, 'dp'), may hold values from -0.25 to 0.25
- norm_gain: bfloat16 [2, 1280], P(None, 'dp'), may hold values from 0.5 to 1.5
Outputs:
- encoded: bfloat16 [512, 128, 1280], P(('grp', 'dp'))
- block_grad: bfloat16 [512, 128, 1280], P(('grp', 'dp'))
- qkv_grad: float32 [4, 1280, 1920], P('grp', 'dp')
- out_grad: float32 [4, 640, 1280], P('grp', 'dp')
- gain_grad: float32 [4, 1280], P('grp', 'dp')
The draws below stay inside these ranges and needn't reach their ends.
Inputs may be any that keep to these rules, and one draw needn't show every extreme that they name: On one index of dp, chosen by the draw, all blocks of all four grp rows have the same modality. `time_rank`: within each device's 4 blocks, a permutation of 0 to 3.
All inputs are finite; a program needn't handle non-finite values.
Results may differ from the reference program's by a relative error of at most 0.029.
The reference program's roundings to bfloat16 on the way count: a program that leaves them out, or rounds other values in their place, can miss the bound.
Values may be sent and summed in bfloat16 or wider, within the bound.
A program may use at most 128 MiB of HBM per device.

```python
import math
import jax
import jax.numpy as jnp
from jax import lax

D = 1280
A_HEADS = 10
A_SIZE = 64
V_HEADS = 8
V_SIZE = 80
INNER = 640
WIN = 128
VWIN = 64
NB = 4
NBLK = 512
N_GRP = 4
N_DP = 32


def draw_modality(key, part):
    key = jax.random.fold_in(key, 11)
    key_row, key_kind, key_base = jax.random.split(key, 3)
    chosen = jax.random.randint(key_row, (), 0, N_DP)
    fixed_kind = jax.random.randint(key_kind, (), 0, 2)
    base = jax.random.randint(key_base, (NBLK,), 0, 2)
    device_dp = jnp.arange(NBLK) // NB % N_DP
    return jnp.where(device_dp == chosen, fixed_kind, base).astype(jnp.int32)


def draw_time_rank(key, part):
    key = jax.random.fold_in(key, 23)
    owner_keys = jax.random.split(key, NBLK // NB)
    ranks = jax.vmap(lambda one_key: jax.random.permutation(one_key, NB))(owner_keys)
    return ranks.reshape(-1).astype(jnp.int32)


def draw_blocks(key, part):
    key = jax.random.fold_in(key, 5)
    array_shape = (NBLK, WIN, D)
    values_drawn = jax.random.truncated_normal(key, -6.0, 6.0, array_shape, jnp.float32)
    pair_count = max(1, VWIN // 8)
    position = jnp.arange(WIN)
    in_window = position % VWIN
    copied = (in_window >= VWIN // 2) & (in_window < VWIN // 2 + pair_count)
    source = jnp.where(copied, position - VWIN // 2, position)
    partner = jnp.take(values_drawn, source, axis=1)
    leading = jnp.arange(D) < D // 2
    chosen = copied[:, None] & leading[None, :]
    return jnp.where(chosen[None, :, :], partner, values_drawn).astype(jnp.bfloat16)


def draw_qkv_weight(key, part):
    key = jax.random.fold_in(key, 7)
    key_drawn, key_common, key_noise = jax.random.split(key, 3)
    columns = 3 * INNER
    drawn = jax.random.truncated_normal(key_drawn, -4.0, 4.0, (2, D, columns), jnp.float32) / math.sqrt(D)
    common = jax.random.truncated_normal(key_common, -4.0, 4.0, (2, D, INNER), jnp.float32)
    noise_part = jax.random.truncated_normal(key_noise, -4.0, 4.0, (2, D, columns), jnp.float32) * (0.3 / math.sqrt(D))
    strength = jnp.array([2.0, 2.3], jnp.float32)
    column_index = jnp.arange(columns)
    within = column_index % INNER
    head_width = jnp.array([A_SIZE, V_SIZE], jnp.int32)
    aligned = (column_index[None, :] < 2 * INNER) & (within[None, :] < head_width[:, None])
    leading = (jnp.arange(D) < D // 2).astype(jnp.float32)
    common_full = jnp.take(common, within, axis=2)
    strong = strength[:, None, None] * common_full * leading[None, :, None] / math.sqrt(D // 2) + noise_part
    result = jnp.where(aligned[:, None, :], strong, drawn)
    return jnp.clip(result, -5.0, 5.0).astype(jnp.bfloat16)


def steps_of(stream_key, extent, pieces, least, top_value):
    level, own = 1.0, jax.random.fold_in(stream_key, 6)
    for dim, blocks in pieces:
        draws = jnp.exp(jax.random.uniform(jax.random.fold_in(own, dim), (blocks,), jnp.float32, least / len(pieces), top_value / len(pieces)))
        level = level * jnp.repeat(draws, extent[dim] // blocks).reshape([-1 if axis == dim else 1 for axis in range(len(extent))])
    return level


def gaussian(own_key, dims, spread, bound, cuts=(), held_as=jnp.bfloat16):
    entries = spread * jax.random.normal(own_key, dims, jnp.float32)
    if cuts:
        entries = entries * steps_of(own_key, dims, cuts, -0.22, 0.18)
    return jnp.clip(entries, -bound, bound).astype(held_as)


def setup_inputs(seed: int = 0) -> dict:
    streams_of = jax.random.split(jax.random.key(seed), 8)
    return {
        "blocks": draw_blocks(jax.random.fold_in(streams_of[7], 71), 0),
        "cotangent": gaussian(streams_of[1], (NBLK, WIN, D), 1.0, 6.0, ((0, 128),)),
        "modality": draw_modality(jax.random.fold_in(streams_of[7], 71), 0),
        "time_rank": draw_time_rank(jax.random.fold_in(streams_of[7], 71), 0),
        "qkv_weight": draw_qkv_weight(jax.random.fold_in(streams_of[7], 71), 0),
        "out_weight": gaussian(streams_of[5], (2, INNER, D), INNER ** -0.5, 0.25, ((1, 32),)),
        "norm_gain": jnp.clip(1.0 + 0.1 * jax.random.normal(streams_of[6], (2, D), jnp.float32), 0.5, 1.5).astype(jnp.bfloat16),
    }


EPSILON = 1e-05

def attend(qkv_rows, out_cot, heads, head_size, window):
    total_rows = qkv_rows.shape[0]
    inner = heads * head_size
    windows = total_rows // window
    shape = (windows, window, heads, head_size)
    query = qkv_rows[:, :inner].reshape(shape).astype(jnp.float32)
    keys = qkv_rows[:, inner:2 * inner].reshape(shape).astype(jnp.float32)
    values = qkv_rows[:, 2 * inner:].reshape(shape).astype(jnp.float32)
    scale = 1.0 / math.sqrt(head_size)
    scores = jnp.einsum('wqhd,wkhd->whqk', query, keys) * scale
    row_max = lax.optimization_barrier(jnp.max(scores, axis=-1, keepdims=True))
    exponent = jnp.exp(scores - row_max)
    probs = exponent / lax.optimization_barrier(jnp.sum(exponent, axis=-1, keepdims=True))
    probs_low = probs.astype(jnp.bfloat16)
    probs_wide = probs_low.astype(jnp.float32)
    mixed = jnp.einsum('whqk,wkhd->wqhd', probs_wide, values).astype(jnp.bfloat16).reshape(total_rows, inner)
    cot_heads = out_cot.reshape(shape).astype(jnp.float32)
    d_probs = jnp.einsum('wqhd,wkhd->whqk', cot_heads, values)
    d_values = jnp.einsum('whqk,wqhd->wkhd', probs_wide, cot_heads).astype(jnp.bfloat16)
    d_scores = (probs * (d_probs - lax.optimization_barrier(jnp.sum(d_probs * probs, axis=-1, keepdims=True))) * scale).astype(jnp.bfloat16)
    d_wide = d_scores.astype(jnp.float32)
    d_query = jnp.einsum('whqk,wkhd->wqhd', d_wide, keys).astype(jnp.bfloat16)
    d_keys = jnp.einsum('whqk,wqhd->wkhd', d_wide, query).astype(jnp.bfloat16)
    d_qkv = jnp.concatenate([d_query.reshape(total_rows, inner), d_keys.reshape(total_rows, inner), d_values.reshape(total_rows, inner)], axis=1)
    return (mixed, d_qkv)

def audio_attend(qkv_rows, out_cot):
    return attend(qkv_rows, out_cot, A_HEADS, A_SIZE, WIN)

def vision_attend(qkv_rows, out_cot):
    return attend(qkv_rows, out_cot, V_HEADS, V_SIZE, VWIN)

def encode(x_rows, cot_rows, w_qkv, w_out, gain, kind_index):
    x_float = x_rows.astype(jnp.float32)
    mean_row = lax.optimization_barrier(jnp.mean(x_float, axis=-1, keepdims=True))
    centered = x_float - mean_row
    inverse = lax.rsqrt(lax.optimization_barrier(jnp.mean(centered * centered, axis=-1, keepdims=True)) + EPSILON)
    x_hat = centered * inverse
    gain_float = gain.astype(jnp.float32)
    normed = (x_hat * gain_float).astype(jnp.bfloat16)
    qkv_rows = jnp.dot(normed, w_qkv, preferred_element_type=jnp.float32).astype(jnp.bfloat16)
    d_attn = jnp.dot(cot_rows, w_out.T, preferred_element_type=jnp.float32).astype(jnp.bfloat16)
    mixed, d_qkv = lax.cond(kind_index == 0, audio_attend, vision_attend, qkv_rows, d_attn)
    output = (x_float + jnp.dot(mixed, w_out, preferred_element_type=jnp.float32)).astype(jnp.bfloat16)
    grad_out = jnp.dot(mixed.T, cot_rows, preferred_element_type=jnp.float32)
    grad_qkv = jnp.dot(normed.T, d_qkv, preferred_element_type=jnp.float32)
    d_normed = jnp.dot(d_qkv, w_qkv.T, preferred_element_type=jnp.float32)
    grad_gain = lax.optimization_barrier(jnp.sum(d_normed * x_hat, axis=0))
    scaled = d_normed * gain_float
    d_input = inverse * (scaled - lax.optimization_barrier(jnp.mean(scaled, axis=-1, keepdims=True)) - x_hat * lax.optimization_barrier(jnp.mean(scaled * x_hat, axis=-1, keepdims=True)))
    input_grad = (cot_rows.astype(jnp.float32) + d_input).astype(jnp.bfloat16)
    return (output, input_grad, grad_qkv, grad_out, grad_gain)

def reference(blocks, cotangent, modality, time_rank, qkv_weight, out_weight, norm_gain):

    def one_block(carry, item):
        x_rows, cot_rows, kind_index = item
        output, input_grad, grad_qkv, grad_out, grad_gain = encode(x_rows, cot_rows, qkv_weight[kind_index], out_weight[kind_index], norm_gain[kind_index], kind_index)
        carry = (carry[0].at[kind_index].add(grad_qkv), carry[1].at[kind_index].add(grad_out), carry[2].at[kind_index].add(grad_gain))
        return (carry, (output, input_grad))
    start = (jnp.zeros((2, D, 3 * INNER), jnp.float32), jnp.zeros((2, INNER, D), jnp.float32), jnp.zeros((2, D), jnp.float32))
    totals, (outputs, input_grads) = lax.scan(one_block, start, (blocks, cotangent, modality))
    owners = N_GRP * N_DP
    ranks = time_rank.reshape(owners, NB)

    def place(rank_row, values):
        return jnp.zeros_like(values).at[rank_row].set(values)
    encoded = jax.vmap(place)(ranks, outputs.reshape(owners, NB, WIN, D)).reshape(NBLK, WIN, D)
    block_grad = jax.vmap(place)(ranks, input_grads.reshape(owners, NB, WIN, D)).reshape(NBLK, WIN, D)
    select = jnp.arange(N_GRP) // 2
    return (encoded, block_grad, totals[0][select], totals[1][select], totals[2][select])
```

```python
import math

import jax
import jax.numpy as jnp
from jax import lax
from jax.experimental import pallas as pl
from jax.experimental.pallas import tpu as pltpu
from jax.sharding import PartitionSpec as P

A_HEADS = 10
A_SIZE = 64
V_HEADS = 8
V_SIZE = 80
WIN = 128
VWIN = 64
LANES = 128
EPSILON = 1e-05
VMEM_BYTES = 60 * 1024 * 1024


def normalized(x):
    mean_row = jnp.mean(x, axis=-1, keepdims=True)
    centered = x - mean_row
    inverse = lax.rsqrt(jnp.mean(centered * centered, axis=-1, keepdims=True) + EPSILON)
    return centered * inverse, inverse


def nt_dot(a, b):
    return lax.dot_general(a, b, (((1,), (1,)), ((), ())), preferred_element_type=jnp.float32)


def tn_dot(a, b):
    return lax.dot_general(a, b, (((0,), (0,)), ((), ())), preferred_element_type=jnp.float32)


def nn_dot(a, b):
    return jnp.dot(a, b, preferred_element_type=jnp.float32)


def attend_pair(query, keys, values, cot, first, second, scale, same_window):
    zero = jnp.zeros((), jnp.bfloat16)

    def stacked(rows):
        return jnp.concatenate(
            [jnp.where(first, rows, zero), jnp.where(second, rows, zero)], axis=0
        )

    query_two = stacked(query)
    cot_two = stacked(cot)
    scores = nt_dot(query_two, keys) * scale
    if same_window is not None:
        scores = jnp.where(same_window, scores, -1e30)
    row_max = jnp.max(scores, axis=-1, keepdims=True)
    exponent = jnp.exp(scores - row_max)
    probs = exponent * (1.0 / jnp.sum(exponent, axis=-1, keepdims=True))
    probs_low = probs.astype(jnp.bfloat16)
    d_probs = nt_dot(cot_two, values)
    inner = jnp.sum(d_probs * probs, axis=-1, keepdims=True)
    d_scores = (probs * (d_probs - inner) * scale).astype(jnp.bfloat16)

    def beside(rows):
        return jnp.concatenate([rows[:WIN], rows[WIN:]], axis=1)

    mixed = nn_dot(beside(probs_low), stacked(values))
    d_values = tn_dot(probs_low, cot_two)
    d_query = nn_dot(beside(d_scores), stacked(keys))
    d_keys = tn_dot(d_scores, query_two)
    return mixed, d_query, d_keys, d_values


def attend_block(heads, size, vision, qkv, cot, out, d_qkv):
    inner = heads * size
    scale = 1.0 / math.sqrt(size)
    same_window = None
    if vision:
        row = lax.broadcasted_iota(jnp.int32, (2 * WIN, WIN), 0)
        col = lax.broadcasted_iota(jnp.int32, (2 * WIN, WIN), 1)
        same_window = (row % WIN) // VWIN == col // VWIN
    tiles = [[None] * (inner // LANES) for _ in range(4)]
    for pair in range(heads // 2):
        low = 2 * pair * size
        start = low // LANES * LANES
        stop = -(-(low + 2 * size) // LANES) * LANES
        lane = lax.broadcasted_iota(jnp.int32, (WIN, stop - start), 1) + start
        first = (lane >= low) & (lane < low + size)
        second = (lane >= low + size) & (lane < low + 2 * size)
        found = attend_pair(
            qkv[:, start:stop],
            qkv[:, inner + start : inner + stop],
            qkv[:, 2 * inner + start : 2 * inner + stop],
            cot[:, start:stop],
            first,
            second,
            scale,
            same_window,
        )
        for which in range(4):
            for tile in range(start // LANES, stop // LANES):
                at = tile * LANES - start
                part = found[which][:, at : at + LANES]
                held = tiles[which][tile]
                tiles[which][tile] = part if held is None else held + part
        done = range(start // LANES, (low + 2 * size) // LANES)
        for tile in done:
            at = slice(tile * LANES, (tile + 1) * LANES)
            out[:, at] = tiles[0][tile].astype(jnp.bfloat16)
            for which in range(3):
                to = slice(which * inner + tile * LANES, which * inner + (tile + 1) * LANES)
                d_qkv[:, to] = tiles[which + 1][tile].astype(jnp.bfloat16)


def encode_kernel(
    kind_ref,
    rank_ref,
    x_ref,
    cot_ref,
    wq_ref,
    wo_ref,
    gain_ref,
    enc_ref,
    grad_ref,
    dwq_ref,
    dwo_ref,
    dgain_ref,
    qkv_s,
    dattn_s,
    mixed_s,
    dqkv_s,
    ht_s,
    mt_s,
):
    blocks = x_ref.shape[0]
    width = x_ref.shape[2]
    inner = wo_ref.shape[1]
    dgain_ref[...] = jnp.zeros_like(dgain_ref)

    @pl.loop(0, blocks)
    def _(b):
        kind = kind_ref[b]
        rank = rank_ref[b]
        x = x_ref[b].astype(jnp.float32)
        x_hat, inverse = normalized(x)
        gain = gain_ref[kind]
        normed = (x_hat * gain).astype(jnp.bfloat16)
        columns = pl.ds(pl.multiple_of(b * WIN, WIN), WIN)
        turned = normed.T
        for m in range(2):
            ht_s[m, :, columns] = jnp.where(kind == m, turned, jnp.zeros_like(turned))
        for at in range(0, 3 * inner, inner):
            qkv_s[:, at : at + inner] = nn_dot(normed, wq_ref[kind, :, at : at + inner]).astype(
                jnp.bfloat16
            )
        cot = cot_ref[b]
        dattn_s[...] = nt_dot(cot, wo_ref[kind]).astype(jnp.bfloat16)
        d_qkv = dqkv_s.at[b]

        @pl.when(kind == 0)
        def _():
            attend_block(A_HEADS, A_SIZE, False, qkv_s, dattn_s, mixed_s, d_qkv)

        @pl.when(kind != 0)
        def _():
            attend_block(V_HEADS, V_SIZE, True, qkv_s, dattn_s, mixed_s, d_qkv)

        mixed = mixed_s[...]
        mixed_t = mixed.T
        for m in range(2):
            mt_s[m, :, columns] = jnp.where(kind == m, mixed_t, jnp.zeros_like(mixed_t))
        enc_ref[rank] = (x + nn_dot(mixed, wo_ref[kind])).astype(jnp.bfloat16)
        d_normed = nt_dot(dqkv_s[b], wq_ref[kind])
        dgain_ref[kind] += jnp.sum(d_normed * x_hat, axis=0, keepdims=True)
        scaled = d_normed * gain
        d_input = inverse * (
            scaled
            - jnp.mean(scaled, axis=-1, keepdims=True)
            - x_hat * jnp.mean(scaled * x_hat, axis=-1, keepdims=True)
        )
        grad_ref[rank] = (cot.astype(jnp.float32) + d_input).astype(jnp.bfloat16)

    cot_all = cot_ref[...].reshape(blocks * WIN, width)
    d_qkv_all = dqkv_s[...].reshape(blocks * WIN, 3 * inner)

    @pl.loop(0, 2)
    def _(m):
        @pl.loop(0, width, step=256)
        def _(r):
            rows = pl.ds(pl.multiple_of(r, 256), 256)
            dwq_ref[m, rows, :] = nn_dot(ht_s[m, rows, :], d_qkv_all).astype(jnp.bfloat16)

        @pl.loop(0, inner, step=128)
        def _(r):
            rows = pl.ds(pl.multiple_of(r, 128), 128)
            dwo_ref[m, rows, :] = nn_dot(mt_s[m, rows, :], cot_all).astype(jnp.bfloat16)


def encode_own(kind, rank, blocks, cotangent, w_qkv, w_out, gain):
    count, window, width = blocks.shape
    inner = w_out.shape[1]
    tokens = count * window
    bf16, f32 = jnp.bfloat16, jnp.float32
    return pl.pallas_call(
        encode_kernel,
        out_shape=(
            jax.ShapeDtypeStruct(blocks.shape, bf16),
            jax.ShapeDtypeStruct(blocks.shape, bf16),
            jax.ShapeDtypeStruct(w_qkv.shape, bf16),
            jax.ShapeDtypeStruct(w_out.shape, bf16),
            jax.ShapeDtypeStruct((2, 1, width), f32),
        ),
        in_specs=[pl.BlockSpec(memory_space=pltpu.SMEM)] * 2
        + [pl.BlockSpec(memory_space=pltpu.VMEM)] * 5,
        out_specs=(pl.BlockSpec(memory_space=pltpu.VMEM),) * 5,
        scratch_shapes=[
            pltpu.VMEM((window, 3 * inner), bf16),
            pltpu.VMEM((window, inner), bf16),
            pltpu.VMEM((window, inner), bf16),
            pltpu.VMEM((count, window, 3 * inner), bf16),
            pltpu.VMEM((2, width, tokens), bf16),
            pltpu.VMEM((2, inner, tokens), bf16),
        ],
        compiler_params=pltpu.CompilerParams(vmem_limit_bytes=VMEM_BYTES),
    )(kind, rank, blocks, cotangent, w_qkv, w_out, gain.astype(f32)[:, None, :])


def shards(blocks, cotangent, modality, time_rank, qkv_weight, out_weight, norm_gain):
    w_qkv = lax.all_gather(qkv_weight, "dp", axis=1, tiled=True)
    w_out = lax.all_gather(out_weight, "dp", axis=1, tiled=True)
    gain = lax.all_gather(norm_gain, "dp", axis=1, tiled=True)
    encoded, block_grad, d_qkv, d_out, d_gain = encode_own(
        modality, time_rank, blocks, cotangent, w_qkv, w_out, gain
    )
    kind = lax.axis_index("grp") // 2

    def shared(grad):
        part = lax.psum_scatter(grad.astype(jnp.float32), "dp", scatter_dimension=1, tiled=True)
        return lax.dynamic_index_in_dim(lax.psum(part, "grp"), kind, 0, keepdims=True)

    return (encoded, block_grad, shared(d_qkv), shared(d_out), shared(d_gain[:, 0, :]))


def solution(mesh):
    return jax.shard_map(
        shards,
        mesh=mesh,
        in_specs=(
            P(("grp", "dp"), None, None),
            P(("grp", "dp"), None, None),
            P(("grp", "dp")),
            P(("grp", "dp")),
            P(None, "dp", None),
            P(None, "dp", None),
            P(None, "dp"),
        ),
        out_specs=(
            P(("grp", "dp"), None, None),
            P(("grp", "dp"), None, None),
            P("grp", "dp", None),
            P("grp", "dp", None),
            P("grp", "dp"),
        ),
        check_vma=False,
    )
```

```python
import math

import jax
import jax.numpy as jnp
from jax import lax
from jax.experimental import pallas as pl
from jax.experimental.pallas import tpu as pltpu
from jax.sharding import PartitionSpec as P

A_HEADS = 10
A_SIZE = 64
V_HEADS = 8
V_SIZE = 80
WIN = 128
VWIN = 64
LANES = 128
EPSILON = 1e-05
VMEM_BYTES = 60 * 1024 * 1024
RING = 4
STEPS = 12
MESH = pl.DeviceIdType.MESH


def normalized(x):
    mean_row = jnp.mean(x, axis=-1, keepdims=True)
    centered = x - mean_row
    inverse = lax.rsqrt(jnp.mean(centered * centered, axis=-1, keepdims=True) + EPSILON)
    return centered * inverse, inverse


def nt_dot(a, b):
    return lax.dot_general(a, b, (((1,), (1,)), ((), ())), preferred_element_type=jnp.float32)


def tn_dot(a, b):
    return lax.dot_general(a, b, (((0,), (0,)), ((), ())), preferred_element_type=jnp.float32)


def nn_dot(a, b):
    return jnp.dot(a, b, preferred_element_type=jnp.float32)


def attend_pair(query, keys, values, cot, first, second, scale, same_window):
    zero = jnp.zeros((), jnp.bfloat16)

    def stacked(rows):
        return jnp.concatenate(
            [jnp.where(first, rows, zero), jnp.where(second, rows, zero)], axis=0
        )

    query_two = stacked(query)
    cot_two = stacked(cot)
    scores = nt_dot(query_two, keys) * scale
    if same_window is not None:
        scores = jnp.where(same_window, scores, -1e30)
    row_max = jnp.max(scores, axis=-1, keepdims=True)
    exponent = jnp.exp(scores - row_max)
    probs = exponent * (1.0 / jnp.sum(exponent, axis=-1, keepdims=True))
    probs_low = probs.astype(jnp.bfloat16)
    d_probs = nt_dot(cot_two, values)
    inner = jnp.sum(d_probs * probs, axis=-1, keepdims=True)
    d_scores = (probs * (d_probs - inner) * scale).astype(jnp.bfloat16)

    def beside(rows):
        return jnp.concatenate([rows[:WIN], rows[WIN:]], axis=1)

    mixed = nn_dot(beside(probs_low), stacked(values))
    d_values = tn_dot(probs_low, cot_two)
    d_query = nn_dot(beside(d_scores), stacked(keys))
    d_keys = tn_dot(d_scores, query_two)
    return mixed, d_query, d_keys, d_values


def attend_block(heads, size, vision, qkv, cot, out, d_qkv):
    inner = heads * size
    scale = 1.0 / math.sqrt(size)
    same_window = None
    if vision:
        row = lax.broadcasted_iota(jnp.int32, (2 * WIN, WIN), 0)
        col = lax.broadcasted_iota(jnp.int32, (2 * WIN, WIN), 1)
        same_window = (row % WIN) // VWIN == col // VWIN
    tiles = [[None] * (inner // LANES) for _ in range(4)]
    for pair in range(heads // 2):
        low = 2 * pair * size
        start = low // LANES * LANES
        stop = -(-(low + 2 * size) // LANES) * LANES
        lane = lax.broadcasted_iota(jnp.int32, (WIN, stop - start), 1) + start
        first = (lane >= low) & (lane < low + size)
        second = (lane >= low + size) & (lane < low + 2 * size)
        found = attend_pair(
            qkv[:, start:stop],
            qkv[:, inner + start : inner + stop],
            qkv[:, 2 * inner + start : 2 * inner + stop],
            cot[:, start:stop],
            first,
            second,
            scale,
            same_window,
        )
        for which in range(4):
            for tile in range(start // LANES, stop // LANES):
                at = tile * LANES - start
                part = found[which][:, at : at + LANES]
                held = tiles[which][tile]
                tiles[which][tile] = part if held is None else held + part
        done = range(start // LANES, (low + 2 * size) // LANES)
        for tile in done:
            at = slice(tile * LANES, (tile + 1) * LANES)
            out[:, at] = tiles[0][tile].astype(jnp.bfloat16)
            for which in range(3):
                to = slice(which * inner + tile * LANES, which * inner + (tile + 1) * LANES)
                d_qkv[:, to] = tiles[which + 1][tile].astype(jnp.bfloat16)


def encode_kernel(
    kind_ref,
    rank_ref,
    x_ref,
    cot_ref,
    wq_ref,
    packed_ref,
    enc_ref,
    grad_ref,
    dwq_ref,
    dpacked_ref,
    wo_ref,
    gain_ref,
    dgain_ref,
    qkv_s,
    dattn_s,
    mixed_s,
    dqkv_s,
    ht_s,
    mt_s,
):
    blocks = x_ref.shape[0]
    width = x_ref.shape[2]
    inner = wo_ref.shape[1]
    count, padded = packed_ref.shape[1:3]
    rows = inner // count
    dgain_ref[...] = jnp.zeros_like(dgain_ref)

    @pl.loop(0, 2)
    def _(m):
        for at in range(0, count, 4):
            four = [packed_ref[m, at + j, 0:rows].astype(jnp.float32) for j in range(4)]
            wo_ref[m, at * rows : (at + 4) * rows] = jnp.concatenate(four, axis=0).astype(
                jnp.bfloat16
            )
        gain_ref[m] = sum(
            packed_ref[m, at, rows : rows + 1].astype(jnp.float32) for at in range(count)
        )

    @pl.loop(0, blocks)
    def _(b):
        kind = kind_ref[b]
        rank = rank_ref[b]
        x = x_ref[b].astype(jnp.float32)
        x_hat, inverse = normalized(x)
        gain = gain_ref[kind]
        normed = (x_hat * gain).astype(jnp.bfloat16)
        columns = pl.ds(pl.multiple_of(b * WIN, WIN), WIN)
        turned = normed.T
        for m in range(2):
            ht_s[m, :, columns] = jnp.where(kind == m, turned, jnp.zeros_like(turned))
        for at in range(0, 3 * inner, inner):
            qkv_s[:, at : at + inner] = nn_dot(normed, wq_ref[kind, :, at : at + inner]).astype(
                jnp.bfloat16
            )
        cot = cot_ref[b]
        dattn_s[...] = nt_dot(cot, wo_ref[kind]).astype(jnp.bfloat16)
        d_qkv = dqkv_s.at[b]

        @pl.when(kind == 0)
        def _():
            attend_block(A_HEADS, A_SIZE, False, qkv_s, dattn_s, mixed_s, d_qkv)

        @pl.when(kind != 0)
        def _():
            attend_block(V_HEADS, V_SIZE, True, qkv_s, dattn_s, mixed_s, d_qkv)

        mixed = mixed_s[...]
        mixed_t = mixed.T
        for m in range(2):
            mt_s[m, :, columns] = jnp.where(kind == m, mixed_t, jnp.zeros_like(mixed_t))
        enc_ref[rank] = (x + nn_dot(mixed, wo_ref[kind])).astype(jnp.bfloat16)
        d_normed = nt_dot(dqkv_s[b], wq_ref[kind])
        dgain_ref[kind] += jnp.sum(d_normed * x_hat, axis=0, keepdims=True)
        scaled = d_normed * gain
        d_input = inverse * (
            scaled
            - jnp.mean(scaled, axis=-1, keepdims=True)
            - x_hat * jnp.mean(scaled * x_hat, axis=-1, keepdims=True)
        )
        grad_ref[rank] = (cot.astype(jnp.float32) + d_input).astype(jnp.bfloat16)

    cot_all = cot_ref[...].reshape(blocks * WIN, width)
    d_qkv_all = dqkv_s[...].reshape(blocks * WIN, 3 * inner)

    @pl.loop(0, 2)
    def _(m):
        @pl.loop(0, width, step=256)
        def _(r):
            rows = pl.ds(pl.multiple_of(r, 256), 256)
            dwq_ref[m, rows, :] = nn_dot(ht_s[m, rows, :], d_qkv_all).astype(jnp.bfloat16)

        below = jnp.concatenate(
            [dgain_ref[m], jnp.zeros((padded - rows - 1, width), jnp.float32)], axis=0
        )
        for at in range(0, count, 8):
            eight = nn_dot(mt_s[m, at * rows : (at + 8) * rows, :], cot_all)
            for j in range(8):
                one = jnp.concatenate([eight[j * rows : (j + 1) * rows], below], axis=0)
                dpacked_ref[m, at + j] = one.astype(jnp.bfloat16)


def encode_own(kind, rank, blocks, cotangent, w_qkv, packed):
    count, window, width = blocks.shape
    inner = w_qkv.shape[2] // 3
    tokens = count * window
    bf16, f32 = jnp.bfloat16, jnp.float32
    return pl.pallas_call(
        encode_kernel,
        out_shape=(
            jax.ShapeDtypeStruct(blocks.shape, bf16),
            jax.ShapeDtypeStruct(blocks.shape, bf16),
            jax.ShapeDtypeStruct(w_qkv.shape, bf16),
            jax.ShapeDtypeStruct(packed.shape, bf16),
        ),
        in_specs=[pl.BlockSpec(memory_space=pltpu.SMEM)] * 2
        + [pl.BlockSpec(memory_space=pltpu.VMEM)] * 4,
        out_specs=(pl.BlockSpec(memory_space=pltpu.VMEM),) * 4,
        scratch_shapes=[
            pltpu.VMEM((2, inner, width), bf16),
            pltpu.VMEM((2, 1, width), f32),
            pltpu.VMEM((2, 1, width), f32),
            pltpu.VMEM((window, 3 * inner), bf16),
            pltpu.VMEM((window, inner), bf16),
            pltpu.VMEM((window, inner), bf16),
            pltpu.VMEM((count, window, 3 * inner), bf16),
            pltpu.VMEM((2, width, tokens), bf16),
            pltpu.VMEM((2, inner, tokens), bf16),
        ],
        compiler_params=pltpu.CompilerParams(vmem_limit_bytes=VMEM_BYTES),
    )(kind, rank, blocks, cotangent, w_qkv, packed)


def place_of(index):
    return index // (2 * RING), index // 2 % RING, index % 2


def device_at(y, z, core):
    return (lax.axis_index("grp"), (y * RING + z) * 2 + core)


def step_on(position, by):
    return lax.rem(position + by + RING, RING)


def meet(peers):
    barrier = pltpu.get_barrier_semaphore()
    for peer in peers:
        pl.semaphore_signal(barrier, inc=1, device_id=peer, device_id_type=MESH)
    pl.semaphore_wait(barrier, len(peers))


def gather_kernel(wq_in, wo_in, wq, wo, send_sem, recv_sem, own_sem):
    y, z, core = place_of(lax.axis_index("dp"))
    sibling = device_at(y, z, 1 - core)
    meet(
        [device_at(step_on(y, by), z, core) for by in (1, -1)]
        + [device_at(y, step_on(z, by), core) for by in (1, -1)]
        + [sibling]
    )
    sent = []

    class Half:
        def __init__(self, number, kind, source, target, cut):
            self.base = number * STEPS
            self.kind, self.source, self.target, self.cut = kind, source, target, cut
            self.first, self.second = (y, z) if kind == 0 else (z, y)

        def to(self, first_by, second_by):
            first, second = step_on(self.first, first_by), step_on(self.second, second_by)
            return device_at(first, second, core) if self.kind == 0 else device_at(second, first, core)

        def slot(self, first_by):
            first = step_on(self.first, first_by)
            if self.kind == 0:
                return self.target.at[0, first, self.second, core]
            return self.target.at[1, self.second, first, core]

        def half_slot(self, first_by, upper):
            size = self.target.shape[-1] - self.cut if upper else self.cut
            low = self.cut if upper else 0
            first = step_on(self.first, first_by)
            if self.kind == 0:
                return self.target.at[0, first, self.second, core, :, pl.ds(low, size)]
            return self.target.at[1, self.second, first, core, :, pl.ds(low, size)]

        def ring(self, second_by, part=slice(0, RING), at_core=None):
            second = step_on(self.second, second_by)
            at_core = core if at_core is None else at_core
            if self.kind == 0:
                return self.target.at[0, part, second, at_core]
            return self.target.at[1, second, part, at_core]

        def copy(self, number, source, target, device):
            return pltpu.make_async_remote_copy(
                src_ref=source,
                dst_ref=target,
                send_sem=send_sem.at[self.base + number],
                recv_sem=recv_sem.at[self.base + number],
                device_id=device,
                device_id_type=MESH,
            )

        def send(self, number, view, device, source=None):
            one = self.copy(number, view if source is None else source, view, device)
            one.start()
            sent.append(one)

        def arrive(self, number, view):
            self.copy(number, view, view, sibling).wait_recv()

    halves = []
    for source, target, cut in ((wo_in, wo, wo.shape[-1] // 2), (wq_in, wq, 1024)):
        for kind in range(2):
            halves.append(Half(len(halves), kind, source, target, cut))
    own = []
    for number, half in enumerate(halves):
        mine = half.source.at[half.kind]
        half.send(0, half.slot(0), half.to(1, 0), mine)
        half.send(1, half.slot(0), half.to(-1, 0), mine)
        kept = pltpu.make_async_copy(mine, half.slot(0), own_sem.at[number])
        kept.start()
        own.append(kept)
    for half in halves:
        half.arrive(0, half.slot(-1))
        half.send(2, half.half_slot(-1, False), half.to(1, 0))
        half.arrive(1, half.slot(1))
        half.send(3, half.half_slot(1, True), half.to(-1, 0))
    low, high = slice(0, RING // 2), slice(RING // 2, RING)
    for half, kept in zip(halves, own):
        half.arrive(2, half.half_slot(2, False))
        half.arrive(3, half.half_slot(2, True))
        kept.wait()
        half.send(4, half.ring(0), half.to(0, 1))
        half.send(5, half.ring(0), half.to(0, -1))
        half.send(6, half.ring(0), sibling)
    for half in halves:
        half.arrive(4, half.ring(-1))
        half.send(7, half.ring(-1, low), half.to(0, 1))
        half.send(8, half.ring(-1), sibling)
        half.arrive(5, half.ring(1))
        half.send(9, half.ring(1, high), half.to(0, -1))
        half.send(10, half.ring(1), sibling)
    for half in halves:
        half.arrive(7, half.ring(2, low))
        half.arrive(9, half.ring(2, high))
        half.send(11, half.ring(2), sibling)
    for half in halves:
        for number, by in ((6, 0), (8, -1), (10, 1), (11, 2)):
            half.arrive(number, half.ring(by, at_core=1 - core))
    for one in sent:
        one.wait_send()


def gather_weights(qkv_weight, packed):
    anywhere = pl.BlockSpec(memory_space=pl.ANY)
    shape = (2, RING, RING, 2)
    return pl.pallas_call(
        gather_kernel,
        out_shape=(
            jax.ShapeDtypeStruct(shape + qkv_weight.shape[1:], jnp.bfloat16),
            jax.ShapeDtypeStruct(shape + packed.shape[1:], jnp.bfloat16),
        ),
        in_specs=[anywhere] * 2,
        out_specs=(anywhere,) * 2,
        scratch_shapes=[
            pltpu.SemaphoreType.DMA((4 * STEPS,)),
            pltpu.SemaphoreType.DMA((4 * STEPS,)),
            pltpu.SemaphoreType.DMA((4,)),
        ],
        compiler_params=pltpu.CompilerParams(collective_id=0, has_side_effects=True),
    )(qkv_weight, packed)


def scatter_kernel(
    dq, do, out_q, out_o, sum_q, sum_o, one_q, one_o, two_q, two_o, three_q, three_o, four_q, four_o,
    row_q, row_o, send_sem, recv_sem,
):
    row = lax.axis_index("grp")
    index = lax.axis_index("dp")
    y, z, core = place_of(index)
    sibling = device_at(y, z, 1 - core)
    across, beside = (RING - 1 - row, index), (row + 1 - 2 * (row % 2), index)
    meet(
        [device_at(step_on(y, by), z, core) for by in (1, -1)]
        + [device_at(y, step_on(z, by), core) for by in (1, -1)]
        + [sibling, across, beside]
    )
    sent = []

    def copy(number, source, target, device):
        return pltpu.make_async_remote_copy(
            src_ref=source,
            dst_ref=target,
            send_sem=send_sem.at[number],
            recv_sem=recv_sem.at[number],
            device_id=device,
            device_id_type=MESH,
        )

    def add(target, *terms):
        @pl.loop(0, target.shape[0])
        def _(i):
            total = target[i].astype(jnp.float32)
            for term in terms:
                total = total + term[i].astype(jnp.float32)
            target[i] = total.astype(jnp.bfloat16)

    class Half:
        def __init__(self, number, kind, source, total, held, cut):
            self.base = number * STEPS
            self.kind, self.source, self.cut = kind, source, cut
            self.total = total.at[kind]
            self.held = [one.at[kind] for one in held]
            self.first, self.second = (y, z) if kind == 0 else (z, y)

        def to(self, first_by, second_by):
            first, second = step_on(self.first, first_by), step_on(self.second, second_by)
            return device_at(first, second, core) if self.kind == 0 else device_at(second, first, core)

        def given(self, by, at_core):
            second = step_on(self.second, by)
            if self.kind == 0:
                return self.source.at[0, :, second, at_core]
            return self.source.at[1, second, :, at_core]

        def ring(self, by):
            return self.total.at[step_on(self.second, by)]

        def pair(self, by, upper):
            return self.total.at[step_on(self.second, by), pl.ds(2 * upper, 2)]

        def one(self, by):
            return self.total.at[self.second, pl.ds(step_on(self.first, by), 1)]

        def part(self, ref, upper):
            low = self.cut if upper else 0
            size = ref.shape[-1] - self.cut if upper else self.cut
            return ref.at[:, :, pl.ds(low, size)]

        def send(self, number, source, target, device):
            made = copy(self.base + number, source, target, device)
            made.start()
            sent.append(made)

        def arrive(self, number, target):
            copy(self.base + number, target, target, sibling).wait_recv()

    arrays = (
        (do, sum_o, (one_o, two_o, three_o, four_o), do.shape[-1] // 2),
        (dq, sum_q, (one_q, two_q, three_q, four_q), 1024),
    )
    halves = []
    for source, total, held, cut in arrays:
        for kind in range(2):
            halves.append(Half(len(halves), kind, source, total, held, cut))
    order = (2, 1, -1, 0)
    for number, by in enumerate(order):
        for half in halves:
            half.send(number, half.given(by, 1 - core), half.ring(by), sibling)

    def take(half, number):
        by = order[number]
        half.arrive(number, half.ring(by))
        add(half.ring(by), half.given(by, core))

    for half in halves:
        one = half.held[0]
        take(half, 0)
        half.send(4, half.pair(2, 0), one.at[0], half.to(0, 1))
        half.send(5, half.pair(2, 1), one.at[1], half.to(0, -1))
    for half in halves:
        one, two = half.held[:2]
        take(half, 1)
        half.arrive(4, one.at[0])
        add(half.pair(1, 0), one.at[0])
        half.send(6, half.ring(1), two.at[0], half.to(0, 1))
        take(half, 2)
        half.arrive(5, one.at[1])
        add(half.pair(-1, 1), one.at[1])
        half.send(7, half.ring(-1), two.at[1], half.to(0, -1))
    for half in halves:
        take(half, 3)
    for half in halves:
        two, three = half.held[1:3]
        half.arrive(6, two.at[0])
        half.arrive(7, two.at[1])
        add(half.ring(0), two.at[0], two.at[1])
        half.send(8, half.part(half.one(2), 0), half.part(three, 0), half.to(1, 0))
        half.send(9, half.part(half.one(2), 1), half.part(three, 1), half.to(-1, 0))
    for half in halves:
        three, four = half.held[2:]
        half.arrive(8, half.part(three, 0))
        add(half.part(half.one(1), 0), half.part(three, 0))
        half.send(10, half.one(1), four.at[0], half.to(1, 0))
        half.arrive(9, half.part(three, 1))
        add(half.part(half.one(-1), 1), half.part(three, 1))
        half.send(11, half.one(-1), four.at[1], half.to(-1, 0))
    for half in halves:
        four = half.held[3]
        half.arrive(10, four.at[0])
        half.arrive(11, four.at[1])
        add(half.one(0), four.at[0], four.at[1])

    kind = row // 2
    rows = ((sum_o, row_o, out_o, 4 * STEPS), (sum_q, row_q, out_q, 4 * STEPS + 2))

    def own(total, which):
        first = y + (z - y) * which
        second = z + (y - z) * which
        return total.at[which, second, first]

    for total, held, out, number in rows:
        made = copy(number, own(total, 1 - kind), held.at[0], across)
        made.start()
        sent.append(made)
    for total, held, out, number in rows:
        copy(number, held.at[0], held.at[0], sibling).wait_recv()
        mine = own(total, kind)[...].astype(jnp.float32) + held[0].astype(jnp.float32)
        out[...] = mine
        held[1] = mine.astype(jnp.bfloat16)
        made = copy(number + 1, held.at[1], held.at[2], beside)
        made.start()
        sent.append(made)
    for total, held, out, number in rows:
        copy(number + 1, held.at[2], held.at[2], sibling).wait_recv()
        out[...] += held[2].astype(jnp.float32)
    for made in sent:
        made.wait_send()


def scatter_grads(d_qkv, d_packed):
    bf16, f32 = jnp.bfloat16, jnp.float32
    q, o = d_qkv.shape[-2:], d_packed.shape[-2:]
    scratch = []
    for lead in ((2, RING, RING), (2, 2, 2), (2, 2, RING), (2, 1), (2, 2, 1), (3,)):
        scratch += [pltpu.VMEM(lead + q, bf16), pltpu.VMEM(lead + o, bf16)]
    vmem = pl.BlockSpec(memory_space=pltpu.VMEM)
    return pl.pallas_call(
        scatter_kernel,
        out_shape=(jax.ShapeDtypeStruct(q, f32), jax.ShapeDtypeStruct(o, f32)),
        in_specs=[vmem] * 2,
        out_specs=(vmem,) * 2,
        scratch_shapes=scratch
        + [pltpu.SemaphoreType.DMA((4 * STEPS + 4,)), pltpu.SemaphoreType.DMA((4 * STEPS + 4,))],
        compiler_params=pltpu.CompilerParams(
            collective_id=1, has_side_effects=True, vmem_limit_bytes=VMEM_BYTES
        ),
    )(d_qkv, d_packed)


def shards(blocks, cotangent, modality, time_rank, qkv_weight, out_weight, norm_gain):
    rows, width = out_weight.shape[1:]
    share = norm_gain.shape[1]
    start = lax.axis_index("dp") * share
    padded = -(-(rows + 1) // 8) * 8
    packed = jnp.concatenate(
        [
            out_weight,
            lax.dynamic_update_slice(
                jnp.zeros((2, padded - rows, width), jnp.bfloat16), norm_gain[:, None, :], (0, 0, start)
            ),
        ],
        axis=1,
    )
    w_qkv, w_packed = gather_weights(qkv_weight, packed)
    count = 2 * RING * RING
    encoded, block_grad, d_qkv, d_packed = encode_own(
        modality,
        time_rank,
        blocks,
        cotangent,
        w_qkv.reshape(2, width, -1),
        w_packed.reshape(2, count, padded, width),
    )
    share_qkv, share_packed = scatter_grads(d_qkv.reshape(w_qkv.shape), d_packed.reshape(w_packed.shape))
    share_gain = lax.dynamic_slice(share_packed, (rows, start), (1, share))
    return (encoded, block_grad, share_qkv[None], share_packed[None, :rows], share_gain)


def solution(mesh):
    return jax.shard_map(
        shards,
        mesh=mesh,
        in_specs=(
            P(("grp", "dp"), None, None),
            P(("grp", "dp"), None, None),
            P(("grp", "dp")),
            P(("grp", "dp")),
            P(None, "dp", None),
            P(None, "dp", None),
            P(None, "dp"),
        ),
        out_specs=(
            P(("grp", "dp"), None, None),
            P(("grp", "dp"), None, None),
            P("grp", "dp", None),
            P("grp", "dp", None),
            P("grp", "dp"),
        ),
        check_vma=False,
    )
```

```python
import math

import jax
import jax.numpy as jnp
from jax import lax
from jax.experimental import pallas as pl
from jax.experimental.pallas import tpu as pltpu
from jax.sharding import PartitionSpec as P

A_HEADS = 10
A_SIZE = 64
V_HEADS = 8
V_SIZE = 80
WIN = 128
VWIN = 64
LANES = 128
EPSILON = 1e-05
VMEM_BYTES = 62 * 1024 * 1024
RING = 4
CHIPS = RING * RING
STEPS = 35
MESH = pl.DeviceIdType.MESH
OFFSETS = (0, -1, 1, 2)
UP = (True, False, False, True)
BF16, F32 = jnp.bfloat16, jnp.float32


def normalized(x):
    mean_row = jnp.mean(x, axis=-1, keepdims=True)
    centered = x - mean_row
    inverse = lax.rsqrt(jnp.mean(centered * centered, axis=-1, keepdims=True) + EPSILON)
    return centered * inverse, inverse


def nt_dot(a, b):
    return lax.dot_general(a, b, (((1,), (1,)), ((), ())), preferred_element_type=F32)


def tn_dot(a, b):
    return lax.dot_general(a, b, (((0,), (0,)), ((), ())), preferred_element_type=F32)


def nn_dot(a, b):
    return jnp.dot(a, b, preferred_element_type=F32)


def attend_pair(query, keys, values, cot, first, second, scale, same_window):
    zero = jnp.zeros((), BF16)

    def stacked(rows):
        return jnp.concatenate(
            [jnp.where(first, rows, zero), jnp.where(second, rows, zero)], axis=0
        )

    query_two = stacked(query)
    cot_two = stacked(cot)
    scores = jnp.where(same_window, nt_dot(query_two, keys) * scale, -1e30)
    row_max = jnp.max(scores, axis=-1, keepdims=True)
    exponent = jnp.exp(scores - row_max)
    probs = exponent * (1.0 / jnp.sum(exponent, axis=-1, keepdims=True))
    probs_low = probs.astype(BF16)
    d_probs = nt_dot(cot_two, values)
    inner = jnp.sum(d_probs * probs, axis=-1, keepdims=True)
    d_scores = (probs * (d_probs - inner) * scale).astype(BF16)

    def beside(rows):
        return jnp.concatenate([rows[:WIN], rows[WIN:]], axis=1)

    mixed = nn_dot(beside(probs_low), stacked(values))
    d_values = tn_dot(probs_low, cot_two)
    d_query = nn_dot(beside(d_scores), stacked(keys))
    d_keys = tn_dot(d_scores, query_two)
    return mixed, d_query, d_keys, d_values


def attend_block(audio, qkv, cot, out, d_qkv):
    inner = cot.shape[1]
    tile_count = inner // LANES
    scale = jnp.where(audio, 1.0 / math.sqrt(A_SIZE), 1.0 / math.sqrt(V_SIZE)).astype(F32)
    size = jnp.where(audio, A_SIZE, V_SIZE)
    row = lax.broadcasted_iota(jnp.int32, (2 * WIN, WIN), 0)
    col = lax.broadcasted_iota(jnp.int32, (2 * WIN, WIN), 1)
    apart = ((row % WIN) // VWIN != col // VWIN).astype(jnp.int32)
    same_window = apart * jnp.where(audio, 0, 1) == 0
    tiles = [[None] * tile_count for _ in range(4)]
    for pair in range(A_HEADS // 2):
        start, stop = pair * LANES, min((pair + 2) * LANES, inner)
        low = jnp.where(audio, 2 * pair * A_SIZE, 2 * pair * V_SIZE)
        lane = lax.broadcasted_iota(jnp.int32, (WIN, stop - start), 1) + start
        first = (lane >= low) & (lane < low + size)
        second = (lane >= low + size) & (lane < low + 2 * size)
        found = attend_pair(
            qkv[:, start:stop],
            qkv[:, inner + start : inner + stop],
            qkv[:, 2 * inner + start : 2 * inner + stop],
            cot[:, start:stop],
            first,
            second,
            scale,
            same_window,
        )
        for which in range(4):
            for tile in range(start // LANES, stop // LANES):
                at = tile * LANES - start
                part = found[which][:, at : at + LANES]
                held = tiles[which][tile]
                tiles[which][tile] = part if held is None else held + part
        at = slice(start, start + LANES)
        out[:, at] = tiles[0][pair].astype(BF16)
        for which in range(3):
            to = slice(which * inner + start, which * inner + start + LANES)
            d_qkv[:, to] = tiles[which + 1][pair].astype(BF16)


def step_on(position, by):
    return lax.rem(position + by + RING, RING)


class Torus:
    def __init__(self):
        self.row = lax.axis_index("grp")
        self.index = lax.axis_index("dp")
        self.core = self.index % 2
        self.y, self.z = self.index // (2 * RING), self.index // 2 % RING

    def chip(self, first_by, second_by, kind):
        y_by = jnp.where(kind == 0, first_by, second_by)
        z_by = jnp.where(kind == 0, second_by, first_by)
        return step_on(self.y, y_by) * RING + step_on(self.z, z_by)

    def near(self, first_by, second_by):
        return (self.row, self.chip(first_by, second_by, self.core) * 2 + self.core)

    def meet(self):
        self.sibling = (self.row, self.index + 1 - 2 * self.core)
        self.across = (RING - 1 - self.row, self.index)
        self.beside = (self.row + 1 - 2 * (self.row % 2), self.index)
        peers = [self.near(1, 0), self.near(-1, 0), self.near(0, 1), self.near(0, -1)]
        peers += [self.sibling, self.across, self.beside]
        barrier = pltpu.get_barrier_semaphore()
        for peer in peers:
            pl.semaphore_signal(barrier, inc=1, device_id=peer, device_id_type=MESH)
        pl.semaphore_wait(barrier, len(peers))


class Lane:
    def __init__(self, base, send_sem, recv_sem, sibling):
        self.base, self.send_sem, self.recv_sem = base, send_sem, recv_sem
        self.sibling = sibling
        self.sent = []

    def copy(self, number, source, target, device):
        return pltpu.make_async_remote_copy(
            src_ref=source,
            dst_ref=target,
            send_sem=self.send_sem.at[self.base + number],
            recv_sem=self.recv_sem.at[self.base + number],
            device_id=device,
            device_id_type=MESH,
        )

    def send(self, number, source, target, device):
        made = self.copy(number, source, target, device)
        made.start()
        self.sent.append(made)

    def arrive(self, number, target):
        self.copy(number, target, target, self.sibling).wait_recv()

    def finish(self):
        for made in self.sent:
            made.wait_send()
        self.sent = []


class Gather(Lane):
    def __init__(self, base, send_sem, recv_sem, torus, held, cut):
        super().__init__(base, send_sem, recv_sem, torus.sibling)
        self.torus, self.held, self.cut = torus, held, cut

    def slot(self, n, j, kind=None):
        kind = self.torus.core if kind is None else kind
        return self.held.at[kind, self.torus.chip(OFFSETS[n], OFFSETS[j], kind)]

    def half(self, n, upper):
        low = self.cut if upper else 0
        size = self.held.shape[-1] - self.cut if upper else self.cut
        chip = self.torus.chip(OFFSETS[n], 0, self.torus.core)
        return self.held.at[self.torus.core, chip, :, pl.ds(low, size)]

    def pass_on(self, number, view, first_by, second_by):
        self.send(number, view, view, self.torus.near(first_by, second_by))

    def share(self, n, j):
        view = self.slot(n, j)
        self.send(16 + 4 * n + j, view, view, self.sibling)

    def along_second(self, n):
        self.pass_on(4 + 2 * n, self.slot(n, 0), 0, 1)
        self.pass_on(5 + 2 * n, self.slot(n, 0), 0, -1)
        self.share(n, 0)

    def begin(self):
        self.pass_on(0, self.slot(0, 0), 1, 0)
        self.pass_on(1, self.slot(0, 0), -1, 0)
        self.along_second(0)

    def ring_back(self):
        self.arrive(0, self.slot(1, 0))
        self.pass_on(2, self.half(1, False), 1, 0)
        self.along_second(1)

    def ring_ahead(self):
        self.arrive(1, self.slot(2, 0))
        self.pass_on(3, self.half(2, True), -1, 0)
        self.along_second(2)

    def ring_far(self):
        self.arrive(2, self.half(3, False))
        self.arrive(3, self.half(3, True))
        self.along_second(3)

    def second_near(self, n):
        self.arrive(4 + 2 * n, self.slot(n, 1))
        if UP[n]:
            self.pass_on(12 + n, self.slot(n, 1), 0, 1)
        self.share(n, 1)
        self.arrive(5 + 2 * n, self.slot(n, 2))
        if not UP[n]:
            self.pass_on(12 + n, self.slot(n, 2), 0, -1)
        self.share(n, 2)

    def second_far(self, n):
        self.arrive(12 + n, self.slot(n, 3))
        self.share(n, 3)

    def other_kind(self):
        for j in range(4):
            for n in range(4):
                self.arrive(16 + 4 * n + j, self.slot(n, j, 1 - self.torus.core))


class Scatter(Lane):
    def __init__(self, base, send_sem, recv_sem, torus, given, total, held, cut):
        super().__init__(base, send_sem, recv_sem, torus.sibling)
        self.torus, self.given, self.total, self.cut = torus, given, total, cut
        self.one, self.two, self.three, self.four, self.kinds, self.leave, self.row_in = held

    def at(self, n, j):
        return self.torus.chip(OFFSETS[n], OFFSETS[j], self.torus.core)

    def part(self, ref, upper):
        low = self.cut if upper else 0
        size = ref.shape[-1] - self.cut if upper else self.cut
        return ref.at[:, pl.ds(low, size)]

    def add(self, target, *terms):
        value = target[...].astype(F32)
        for term in terms:
            value = value + term[...].astype(F32)
        target[...] = value.astype(BF16)

    def give(self, j):
        for n in range(4):
            chip = self.torus.chip(OFFSETS[n], OFFSETS[j], 1 - self.torus.core)
            self.send(4 * j + n, self.given.at[chip], self.total.at[chip], self.sibling)

    def take(self, j, own):
        for n in range(4):
            chip = self.at(n, j)
            self.arrive(4 * j + n, self.total.at[chip])
            value = own(n, chip) + self.total[chip].astype(F32)
            self.total[chip] = value.astype(BF16)

    def send_far(self):
        for n in range(4):
            device = self.torus.near(0, 1 if UP[n] else -1)
            self.send(16 + n, self.total.at[self.at(n, 3)], self.one.at[n], device)

    def send_near(self, j):
        for n in (3, 1, 2, 0):
            if UP[n] == (j == 2):
                self.arrive(16 + n, self.one.at[n])
                self.add(self.total.at[self.at(n, j)], self.one.at[n])
            number, which = (20 + 2 * n, 0) if j == 2 else (21 + 2 * n, 1)
            device = self.torus.near(0, OFFSETS[j])
            self.send(number, self.total.at[self.at(n, j)], self.two.at[n, which], device)

    def close_second(self, n):
        self.arrive(20 + 2 * n, self.two.at[n, 0])
        self.arrive(21 + 2 * n, self.two.at[n, 1])
        self.add(self.total.at[self.at(n, 0)], self.two.at[n, 0], self.two.at[n, 1])

    def first_far(self):
        self.close_second(3)
        view = self.total.at[self.at(3, 0)]
        self.send(28, self.part(view, False), self.part(self.three, False), self.torus.near(1, 0))
        self.send(29, self.part(view, True), self.part(self.three, True), self.torus.near(-1, 0))
        for n in (2, 1, 0):
            self.close_second(n)

    def first_near(self):
        for n, upper, by in ((2, False, 1), (1, True, -1)):
            view = self.total.at[self.at(n, 0)]
            self.arrive(28 + upper, self.part(self.three, upper))
            self.add(self.part(view, upper), self.part(self.three, upper))
            self.send(30 + upper, view, self.four.at[int(upper)], self.torus.near(by, 0))

    def swap(self, split):
        view = self.total.at[self.at(0, 0)]
        self.arrive(30, self.four.at[0])
        self.arrive(31, self.four.at[1])
        value = view[...].astype(F32) + self.four[0].astype(F32) + self.four[1].astype(F32)
        low, high = split(value)
        core = self.torus.core
        self.kinds[core] = jnp.where(core == 0, low, high).astype(BF16)
        self.leave[...] = jnp.where(core == 0, high, low).astype(BF16)
        self.send(32, self.leave, self.kinds.at[core], self.sibling)

    def cross(self):
        kind = self.torus.row // 2
        self.arrive(32, self.kinds.at[1 - self.torus.core])
        self.send(33, self.kinds.at[1 - kind], self.row_in.at[0], self.torus.across)

    def pair_up(self, out):
        kind = self.torus.row // 2
        self.arrive(33, self.row_in.at[0])
        value = self.kinds[kind].astype(F32) + self.row_in[0].astype(F32)
        out[...] = value
        self.row_in[1] = value.astype(BF16)
        self.send(34, self.row_in.at[1], self.row_in.at[2], self.torus.beside)

    def end(self, out):
        self.arrive(34, self.row_in.at[2])
        out[...] += self.row_in[2].astype(F32)


def layer_kernel(
    kind_ref, rank_ref, x_ref, cot_ref, q_in, o_in, gain_in,
    enc_ref, grad_ref, out_q, out_o,
    wq, wp, wo, gain_s, sib_q, sib_o, sib_gain, xhat_s, inv_s, qkv_s, dattn_s, mixed_s, dqkv_s, ht_s, mt_s,
    y_s, dx_s, dgain_s, give_q, give_o, total_q, total_o, *rest,
):
    held_q, held_o = rest[0:14:2], rest[1:14:2]
    gather_send, gather_recv, scatter_send, scatter_recv = rest[14:]
    blocks, window, width = x_ref.shape
    inner = wo.shape[1]
    rows = inner // CHIPS
    share = width // CHIPS
    padded = wp.shape[2]
    torus = Torus()
    torus.meet()
    core = torus.core
    first = core == 0

    early = Lane(2 * 32, gather_send, gather_recv, torus.sibling)
    early.send(0, o_in.at[1 - core], sib_o, torus.sibling)
    early.send(1, gain_in.at[1 - core], sib_gain, torus.sibling)
    early.send(2, q_in.at[1 - core], sib_q, torus.sibling)
    gather_o = Gather(0, gather_send, gather_recv, torus, wp, width // 2)
    gather_q = Gather(32, gather_send, gather_recv, torus, wq, 1024)
    gathers = (gather_o, gather_q)
    here = torus.y * RING + torus.z
    early.arrive(0, sib_o)
    early.arrive(1, sib_gain)
    mine, other = o_in[core].astype(F32), sib_o[...].astype(F32)
    gain_row = gain_in[core] + sib_gain[...]
    wp[core, here] = jnp.concatenate(
        [
            jnp.where(first, mine, other),
            jnp.where(first, other, mine),
            gain_row,
            jnp.zeros((padded - 2 * mine.shape[0] - 1, width), F32),
        ],
        axis=0,
    ).astype(BF16)
    gather_o.begin()
    early.arrive(2, sib_q)
    mine, other = q_in[core].astype(F32), sib_q[...].astype(F32)
    wq[core, here] = jnp.concatenate(
        [jnp.where(first, mine, other), jnp.where(first, other, mine)], axis=0
    ).astype(BF16)
    gather_q.begin()

    def norm_block(b):
        x_hat, inverse = normalized(x_ref[b].astype(F32))
        xhat_s[b] = x_hat
        inv_s[b] = jnp.broadcast_to(inverse, inv_s.shape[1:])

    norm_block(0)
    for one in gathers:
        one.ring_back()
        one.ring_ahead()
    norm_block(1)
    for one in gathers:
        one.second_near(0)
    norm_block(2)
    for one in gathers:
        one.ring_far()
    norm_block(3)
    for one in gathers:
        one.second_near(1)
        one.second_near(2)
        one.second_far(0)
    for one in gathers:
        one.second_near(3)
        one.second_far(1)
        one.second_far(2)
        one.second_far(3)
    gather_o.other_kind()

    @pl.loop(0, 2)
    def _(m):
        for chip in range(0, CHIPS, 2):
            two = [wp[m, chip + i, 0:rows].astype(F32) for i in range(2)]
            wo[m, chip * rows : (chip + 2) * rows] = jnp.concatenate(two, axis=0).astype(BF16)
        gain_s[m] = sum(wp[m, chip, rows : rows + 1].astype(F32) for chip in range(CHIPS))

    gather_q.other_kind()

    def weights(kind, low, high):
        return wq[kind, :, :, low:high].reshape(width, high - low)

    @pl.loop(0, blocks)
    def _(b):
        kind = kind_ref[b]
        normed = (xhat_s[b] * gain_s[kind]).astype(BF16)
        columns = pl.ds(pl.multiple_of(b * WIN, WIN), WIN)
        turned = normed.T
        for m in range(2):
            ht_s[m, :, columns] = jnp.where(kind == m, turned, jnp.zeros_like(turned))
        for at in range(0, 3 * inner, inner):
            qkv_s[:, at : at + inner] = nn_dot(normed, weights(kind, at, at + inner)).astype(BF16)
        dattn_s[...] = nt_dot(cot_ref[b], wo[kind]).astype(BF16)
        attend_block(kind == 0, qkv_s, dattn_s, mixed_s.at[b], dqkv_s.at[b])
        mixed_t = mixed_s[b].T
        for m in range(2):
            mt_s[m, :, columns] = jnp.where(kind == m, mixed_t, jnp.zeros_like(mixed_t))

    scatter_q = Scatter(
        0, scatter_send, scatter_recv, torus, give_q, total_q, held_q, 1024
    )
    scatter_o = Scatter(
        STEPS, scatter_send, scatter_recv, torus, give_o, total_o, held_o, width // 2
    )
    tokens = blocks * window
    d_qkv_all = dqkv_s[...].reshape(tokens, 3 * inner)

    def q_block(kind, j):
        parts = []
        for n in range(4):
            chip = torus.chip(OFFSETS[n], OFFSETS[j], kind)
            at = pl.ds(pl.multiple_of(chip * share, 16), share)
            parts.append(ht_s[kind, at, :])
        return nn_dot(jnp.concatenate(parts, axis=0), d_qkv_all)

    for j in (3, 2, 1, 0):
        found = q_block(1 - core, j)
        for n in range(4):
            chip = torus.chip(OFFSETS[n], OFFSETS[j], 1 - core)
            give_q[chip] = found[n * share : (n + 1) * share].astype(BF16)
        scatter_q.give(j)

    def take_q(j):
        found = q_block(core, j)
        scatter_q.take(j, lambda n, chip: found[n * share : (n + 1) * share])

    take_q(3)
    scatter_q.send_far()
    take_q(2)
    scatter_q.send_near(2)
    take_q(1)
    scatter_q.send_near(1)
    take_q(0)
    dgain_s[...] = jnp.zeros_like(dgain_s)

    def finish_blocks(low, high):
        @pl.loop(low, high)
        def _(b):
            kind = kind_ref[b]
            x_hat = xhat_s[b]
            gain = gain_s[kind]
            y = x_ref[b].astype(F32) + nn_dot(mixed_s[b], wo[kind])
            y_s[b] = y.astype(BF16)
            d_normed = nt_dot(dqkv_s[b], weights(kind, 0, 3 * inner))
            d_gain = jnp.sum(d_normed * x_hat, axis=0, keepdims=True)
            for m in range(2):
                dgain_s[m] += jnp.where(kind == m, d_gain, jnp.zeros_like(d_gain))
            scaled = d_normed * gain
            d_input = inv_s[b][:, 0:1] * (
                scaled
                - jnp.mean(scaled, axis=-1, keepdims=True)
                - x_hat * jnp.mean(scaled * x_hat, axis=-1, keepdims=True)
            )
            dx_s[b] = (cot_ref[b].astype(F32) + d_input).astype(BF16)

    finish_blocks(0, blocks)
    cot_all = cot_ref[...].reshape(tokens, width)

    def o_rows(kind, store):
        below = jnp.concatenate(
            [dgain_s[kind], jnp.zeros((padded - rows - 1, width), F32)], axis=0
        )
        for at in range(0, CHIPS, 4):
            four = nn_dot(mt_s[kind, at * rows : (at + 4) * rows, :], cot_all)
            for i in range(4):
                store(at + i, jnp.concatenate([four[i * rows : (i + 1) * rows], below], axis=0))

    def store_given(chip, value):
        give_o[chip] = value.astype(BF16)

    o_rows(1 - core, store_given)
    for j in (3, 2, 1, 0):
        scatter_o.give(j)
    scatter_q.first_far()
    gather_o.finish()

    def keep_own(chip, value):
        wp[core, chip] = value.astype(BF16)

    o_rows(core, keep_own)
    scatter_q.first_near()

    def take_o(j):
        scatter_o.take(j, lambda n, chip: wp[core, chip].astype(F32))

    take_o(3)
    scatter_o.send_far()
    scatter_q.swap(lambda value: (value[:share // 2], value[share // 2 :]))
    take_o(2)
    take_o(1)
    scatter_o.send_near(2)
    scatter_o.send_near(1)
    take_o(0)
    scatter_q.cross()
    for r in range(blocks):
        y, dx = y_s[0], dx_s[0]
        for b in range(1, blocks):
            y = jnp.where(rank_ref[b] == r, y_s[b], y)
            dx = jnp.where(rank_ref[b] == r, dx_s[b], dx)
        enc_ref[r] = y
        grad_ref[r] = dx
    scatter_o.first_far()
    scatter_q.pair_up(out_q)
    scatter_o.first_near()

    def split_o(value):
        half = rows // 2
        below = jnp.concatenate([value[rows : rows + 1], jnp.zeros((3, width), F32)], axis=0)
        return (
            jnp.concatenate([value[:half], below], axis=0),
            jnp.concatenate([value[half:rows], below], axis=0),
        )

    scatter_o.swap(split_o)
    scatter_q.end(out_q)
    scatter_o.cross()
    scatter_o.pair_up(out_o)
    scatter_o.end(out_o)
    for one in (early, gather_o, gather_q, scatter_q, scatter_o):
        one.finish()


def layer(kind, rank, blocks, cotangent, qkv_weight, out_weight, gain_row):
    count, window, width = blocks.shape
    inner = qkv_weight.shape[2] // 3
    tokens = count * window
    rows = inner // CHIPS
    padded = -(-(rows + 1) // 16) * 16
    q, o = (width // CHIPS, 3 * inner), (padded, width)
    half_q, half_o = qkv_weight.shape[1:], (-(-(rows // 2 + 1) // 8) * 8, width)
    scratch = [
        pltpu.VMEM((2, CHIPS) + q, BF16),
        pltpu.VMEM((2, CHIPS) + o, BF16),
        pltpu.VMEM((2, inner, width), BF16),
        pltpu.VMEM((2, 1, width), F32),
        pltpu.VMEM(qkv_weight.shape[1:], BF16),
        pltpu.VMEM(out_weight.shape[1:], BF16),
        pltpu.VMEM((1, width), F32),
        pltpu.VMEM((count, window, width), F32),
        pltpu.VMEM((count, window, LANES), F32),
        pltpu.VMEM((window, 3 * inner), BF16),
        pltpu.VMEM((window, inner), BF16),
        pltpu.VMEM((count, window, inner), BF16),
        pltpu.VMEM((count, window, 3 * inner), BF16),
        pltpu.VMEM((2, width, tokens), BF16),
        pltpu.VMEM((2, inner, tokens), BF16),
        pltpu.VMEM((count, window, width), BF16),
        pltpu.VMEM((count, window, width), BF16),
        pltpu.VMEM((2, 1, width), F32),
        pltpu.VMEM((CHIPS,) + q, BF16),
        pltpu.VMEM((CHIPS,) + o, BF16),
        pltpu.VMEM((CHIPS,) + q, BF16),
        pltpu.VMEM((CHIPS,) + o, BF16),
    ]
    for lead in ((4,), (4, 2), (), (2,)):
        scratch += [pltpu.VMEM(lead + q, BF16), pltpu.VMEM(lead + o, BF16)]
    for lead in ((2,), (), (3,)):
        scratch += [pltpu.VMEM(lead + half_q, BF16), pltpu.VMEM(lead + half_o, BF16)]
    scratch += [pltpu.SemaphoreType.DMA((2 * 32 + 3,))] * 2
    scratch += [pltpu.SemaphoreType.DMA((2 * STEPS,))] * 2
    vmem = pl.BlockSpec(memory_space=pltpu.VMEM)
    return pl.pallas_call(
        layer_kernel,
        out_shape=(
            jax.ShapeDtypeStruct(blocks.shape, BF16),
            jax.ShapeDtypeStruct(blocks.shape, BF16),
            jax.ShapeDtypeStruct(half_q, F32),
            jax.ShapeDtypeStruct(half_o, F32),
        ),
        in_specs=[pl.BlockSpec(memory_space=pltpu.SMEM)] * 2 + [vmem] * 5,
        out_specs=(vmem,) * 4,
        scratch_shapes=scratch,
        compiler_params=pltpu.CompilerParams(
            collective_id=0, has_side_effects=True, vmem_limit_bytes=VMEM_BYTES
        ),
    )(kind, rank, blocks, cotangent, qkv_weight, out_weight, gain_row)


def shards(blocks, cotangent, modality, time_rank, qkv_weight, out_weight, norm_gain):
    rows, width = out_weight.shape[1:]
    share = norm_gain.shape[1]
    start = lax.axis_index("dp") * share
    gain_row = lax.dynamic_update_slice(
        jnp.zeros((2, width), F32), norm_gain.astype(F32), (0, start)
    )[:, None, :]
    encoded, block_grad, share_qkv, share_packed = layer(
        modality, time_rank, blocks, cotangent, qkv_weight, out_weight, gain_row
    )
    share_gain = lax.dynamic_slice(share_packed, (rows, start), (1, share))
    return (encoded, block_grad, share_qkv[None], share_packed[None, :rows], share_gain)


def solution(mesh):
    return jax.shard_map(
        shards,
        mesh=mesh,
        in_specs=(
            P(("grp", "dp"), None, None),
            P(("grp", "dp"), None, None),
            P(("grp", "dp")),
            P(("grp", "dp")),
            P(None, "dp", None),
            P(None, "dp", None),
            P(None, "dp"),
        ),
        out_specs=(
            P(("grp", "dp"), None, None),
            P(("grp", "dp"), None, None),
            P("grp", "dp", None),
            P("grp", "dp", None),
            P("grp", "dp"),
        ),
        check_vma=False,
    )
```

```python
import math

import jax
import jax.numpy as jnp
from jax import lax
from jax.experimental import pallas as pl
from jax.experimental.pallas import tpu as pltpu
from jax.sharding import PartitionSpec as P

A_HEADS = 10
A_SIZE = 64
V_HEADS = 8
V_SIZE = 80
WIN = 128
VWIN = 64
LANES = 128
EPSILON = 1e-05
VMEM_BYTES = 63 * 1024 * 1024
RING = 4
CHIPS = RING * RING
STEPS = 51
BEHIND = 6
AWAY_Q, AWAY_O = 5 * LANES, 3 * LANES
MESH = pl.DeviceIdType.MESH
OFFSETS = (0, -1, 1, 2)
UP = (True, False, False, True)
BF16, F32 = jnp.bfloat16, jnp.float32


def normalized(x):
    mean_row = jnp.mean(x, axis=-1, keepdims=True)
    centered = x - mean_row
    inverse = lax.rsqrt(jnp.mean(centered * centered, axis=-1, keepdims=True) + EPSILON)
    return centered * inverse, inverse


def nt_dot(a, b):
    return lax.dot_general(a, b, (((1,), (1,)), ((), ())), preferred_element_type=F32)


def tn_dot(a, b):
    return lax.dot_general(a, b, (((0,), (0,)), ((), ())), preferred_element_type=F32)


def nn_dot(a, b):
    return jnp.dot(a, b, preferred_element_type=F32)


def attend_pair(query, keys, values, cot, first, second, scale, same_window):
    zero = jnp.zeros((), BF16)

    def stacked(rows):
        return jnp.concatenate(
            [jnp.where(first, rows, zero), jnp.where(second, rows, zero)], axis=0
        )

    query_two = stacked(query)
    cot_two = stacked(cot)
    scores = jnp.where(same_window, nt_dot(query_two, keys) * scale, -1e30)
    row_max = jnp.max(scores, axis=-1, keepdims=True)
    exponent = jnp.exp(scores - row_max)
    probs = exponent * (1.0 / jnp.sum(exponent, axis=-1, keepdims=True))
    probs_low = probs.astype(BF16)
    d_probs = nt_dot(cot_two, values)
    inner = jnp.sum(d_probs * probs, axis=-1, keepdims=True)
    d_scores = (probs * (d_probs - inner) * scale).astype(BF16)

    def beside(rows):
        return jnp.concatenate([rows[:WIN], rows[WIN:]], axis=1)

    mixed = nn_dot(beside(probs_low), stacked(values))
    d_values = tn_dot(probs_low, cot_two)
    d_query = nn_dot(beside(d_scores), stacked(keys))
    d_keys = tn_dot(d_scores, query_two)
    return mixed, d_query, d_keys, d_values


def attend_block(audio, qkv, cot, out, d_qkv):
    inner = cot.shape[1]
    tile_count = inner // LANES
    scale = jnp.where(audio, 1.0 / math.sqrt(A_SIZE), 1.0 / math.sqrt(V_SIZE)).astype(F32)
    size = jnp.where(audio, A_SIZE, V_SIZE)
    row = lax.broadcasted_iota(jnp.int32, (2 * WIN, WIN), 0)
    col = lax.broadcasted_iota(jnp.int32, (2 * WIN, WIN), 1)
    apart = ((row % WIN) // VWIN != col // VWIN).astype(jnp.int32)
    same_window = apart * jnp.where(audio, 0, 1) == 0
    tiles = [[None] * tile_count for _ in range(4)]
    for pair in range(A_HEADS // 2):
        start, stop = pair * LANES, min((pair + 2) * LANES, inner)
        low = jnp.where(audio, 2 * pair * A_SIZE, 2 * pair * V_SIZE)
        lane = lax.broadcasted_iota(jnp.int32, (WIN, stop - start), 1) + start
        first = (lane >= low) & (lane < low + size)
        second = (lane >= low + size) & (lane < low + 2 * size)
        found = attend_pair(
            qkv[:, start:stop],
            qkv[:, inner + start : inner + stop],
            qkv[:, 2 * inner + start : 2 * inner + stop],
            cot[:, start:stop],
            first,
            second,
            scale,
            same_window,
        )
        for which in range(4):
            for tile in range(start // LANES, stop // LANES):
                at = tile * LANES - start
                part = found[which][:, at : at + LANES]
                held = tiles[which][tile]
                tiles[which][tile] = part if held is None else held + part
        at = slice(start, start + LANES)
        out[:, at] = tiles[0][pair].astype(BF16)
        for which in range(3):
            to = slice(which * inner + start, which * inner + start + LANES)
            d_qkv[:, to] = tiles[which + 1][pair].astype(BF16)


def step_on(position, by):
    return lax.rem(position + by + RING, RING)


class Torus:
    def __init__(self):
        self.row = lax.axis_index("grp")
        self.index = lax.axis_index("dp")
        self.core = self.index % 2
        self.y, self.z = self.index // (2 * RING), self.index // 2 % RING

    def chip(self, first_by, second_by, kind):
        y_by = jnp.where(kind == 0, first_by, second_by)
        z_by = jnp.where(kind == 0, second_by, first_by)
        return step_on(self.y, y_by) * RING + step_on(self.z, z_by)

    def near(self, first_by, second_by):
        return (self.row, self.chip(first_by, second_by, self.core) * 2 + self.core)

    def meet(self):
        self.sibling = (self.row, self.index + 1 - 2 * self.core)
        self.across = (RING - 1 - self.row, self.index)
        self.beside = (self.row + 1 - 2 * (self.row % 2), self.index)
        peers = [self.near(1, 0), self.near(-1, 0), self.near(0, 1), self.near(0, -1)]
        peers += [self.sibling, self.across, self.beside]
        barrier = pltpu.get_barrier_semaphore()
        for peer in peers:
            pl.semaphore_signal(barrier, inc=1, device_id=peer, device_id_type=MESH)
        pl.semaphore_wait(barrier, len(peers))


class Lane:
    def __init__(self, base, send_sem, recv_sem, sibling):
        self.base, self.send_sem, self.recv_sem = base, send_sem, recv_sem
        self.sibling = sibling
        self.sent = []

    def copy(self, number, source, target, device):
        return pltpu.make_async_remote_copy(
            src_ref=source,
            dst_ref=target,
            send_sem=self.send_sem.at[self.base + number],
            recv_sem=self.recv_sem.at[self.base + number],
            device_id=device,
            device_id_type=MESH,
        )

    def send(self, number, source, target, device):
        made = self.copy(number, source, target, device)
        made.start()
        self.sent.append(made)

    def arrive(self, number, target):
        self.copy(number, target, target, self.sibling).wait_recv()

    def finish(self):
        for made in self.sent:
            made.wait_send()
        self.sent = []


class Slots(Lane):
    def __init__(self, base, send_sem, recv_sem, torus, columns, away):
        super().__init__(base, send_sem, recv_sem, torus.sibling)
        self.torus, self.away, self.carried = torus, away, columns - away
        odd = torus.row % 2
        self.start = pl.multiple_of(away * (1 - odd), LANES)
        self.missing = pl.ds(pl.multiple_of(self.carried * odd, LANES), away)
        self.lent = pl.ds(pl.multiple_of(self.carried * (1 - odd), LANES), away)
        self.cut = -(-self.carried // (2 * LANES)) * LANES

    def chip(self, n, j):
        return self.torus.chip(OFFSETS[n], OFFSETS[j], self.torus.core)

    def window(self):
        return pl.ds(self.start, self.carried)

    def half_window(self, upper):
        if upper:
            return pl.ds(self.start + self.cut, self.carried - self.cut)
        return pl.ds(self.start, self.cut)

    def neighbour(self, n, j):
        return self.torus.across if (n + j) % 2 else self.torus.beside


class Gather(Slots):
    def __init__(self, base, send_sem, recv_sem, torus, held, away, pending):
        super().__init__(base, send_sem, recv_sem, torus, held.shape[-1], away)
        self.held, self.pending = held, pending

    def slot(self, n, j, columns=None):
        columns = self.window() if columns is None else columns
        return self.held.at[self.torus.core, self.chip(n, j), :, columns]

    def half(self, n, upper):
        return self.slot(n, 0, self.half_window(upper))

    def pass_on(self, number, view, first_by, second_by):
        self.send(number, view, view, self.torus.near(first_by, second_by))

    def share(self, n, j):
        view = self.held.at[self.torus.core, self.chip(n, j)]
        self.send(16 + 4 * n + j, view, view, self.sibling)

    def lend(self, n, j):
        view = self.slot(n, j, self.lent)
        self.send(32 + 4 * n + j, view, view, self.neighbour(n, j))
        self.pending.append((self, n, j))
        if len(self.pending) > BEHIND:
            one, n, j = self.pending.pop(0)
            one.complete(n, j)

    def complete(self, n, j):
        self.arrive(32 + 4 * n + j, self.slot(n, j, self.missing))
        self.share(n, j)

    def along_second(self, n):
        self.pass_on(4 + 2 * n, self.slot(n, 0), 0, 1)
        self.pass_on(5 + 2 * n, self.slot(n, 0), 0, -1)

    def begin(self):
        self.pass_on(0, self.slot(0, 0), 1, 0)
        self.pass_on(1, self.slot(0, 0), -1, 0)
        self.along_second(0)
        self.share(0, 0)

    def ring_back(self):
        self.arrive(0, self.slot(1, 0))
        self.pass_on(2, self.half(1, False), 1, 0)
        self.along_second(1)
        self.lend(1, 0)

    def ring_ahead(self):
        self.arrive(1, self.slot(2, 0))
        self.pass_on(3, self.half(2, True), -1, 0)
        self.along_second(2)
        self.lend(2, 0)

    def ring_far(self):
        self.arrive(2, self.half(3, False))
        self.arrive(3, self.half(3, True))
        self.along_second(3)
        self.lend(3, 0)

    def second_near(self, n):
        self.arrive(4 + 2 * n, self.slot(n, 1))
        if UP[n]:
            self.pass_on(12 + n, self.slot(n, 1), 0, 1)
        self.lend(n, 1)
        self.arrive(5 + 2 * n, self.slot(n, 2))
        if not UP[n]:
            self.pass_on(12 + n, self.slot(n, 2), 0, -1)
        self.lend(n, 2)

    def second_far(self, n):
        self.arrive(12 + n, self.slot(n, 3))
        self.lend(n, 3)

    def other_kind(self):
        other = 1 - self.torus.core
        for j in range(4):
            for n in range(4):
                chip = self.torus.chip(OFFSETS[n], OFFSETS[j], other)
                self.arrive(16 + 4 * n + j, self.held.at[other, chip])


class Scatter(Slots):
    def __init__(self, base, send_sem, recv_sem, torus, given, total, held, away):
        super().__init__(base, send_sem, recv_sem, torus, total.shape[-1], away)
        self.given, self.total = given, total
        self.one, self.two, self.three, self.four, self.lent_in = held[:5]
        self.kinds, self.leave, self.row_in = held[5:]

    def view(self, n, j, columns=None):
        columns = self.window() if columns is None else columns
        return self.total.at[self.chip(n, j), :, columns]

    def part(self, upper):
        return self.three.at[:, slice(self.cut, None) if upper else slice(0, self.cut)]

    def add(self, target, *terms):
        value = target[...].astype(F32)
        for term in terms:
            value = value + term[...].astype(F32)
        target[...] = value.astype(BF16)

    def give(self, j):
        for n in range(4):
            chip = self.torus.chip(OFFSETS[n], OFFSETS[j], 1 - self.torus.core)
            self.send(4 * j + n, self.given.at[chip], self.total.at[chip], self.sibling)

    def take(self, j, own):
        for n in range(4):
            chip = self.chip(n, j)
            self.arrive(4 * j + n, self.total.at[chip])
            value = own(n, chip) + self.total[chip].astype(F32)
            self.total[chip] = value.astype(BF16)
            if n or j:
                lent = self.view(n, j, self.missing)
                self.send(32 + 4 * j + n, lent, self.lent_in.at[4 * j + n], self.neighbour(n, j))

    def take_lent(self, j):
        for n in range(4):
            if n or j:
                self.arrive(32 + 4 * j + n, self.lent_in.at[4 * j + n])
                self.add(self.view(n, j, self.lent), self.lent_in.at[4 * j + n])

    def send_far(self):
        for n in range(4):
            device = self.torus.near(0, 1 if UP[n] else -1)
            self.send(16 + n, self.view(n, 3), self.one.at[n], device)

    def send_near(self, j):
        for n in (3, 1, 2, 0):
            if UP[n] == (j == 2):
                self.arrive(16 + n, self.one.at[n])
                self.add(self.view(n, j), self.one.at[n])
            number, which = (20 + 2 * n, 0) if j == 2 else (21 + 2 * n, 1)
            device = self.torus.near(0, OFFSETS[j])
            self.send(number, self.view(n, j), self.two.at[n, which], device)

    def close_second(self, n):
        self.arrive(20 + 2 * n, self.two.at[n, 0])
        self.arrive(21 + 2 * n, self.two.at[n, 1])
        self.add(self.view(n, 0), self.two.at[n, 0], self.two.at[n, 1])

    def first_far(self):
        self.close_second(3)
        for upper, by in ((False, 1), (True, -1)):
            view = self.view(3, 0, self.half_window(upper))
            self.send(28 + upper, view, self.part(upper), self.torus.near(by, 0))
        for n in (2, 1, 0):
            self.close_second(n)

    def first_near(self):
        for n, upper, by in ((2, False, 1), (1, True, -1)):
            self.arrive(28 + upper, self.part(upper))
            self.add(self.view(n, 0, self.half_window(upper)), self.part(upper))
            self.send(30 + upper, self.view(n, 0), self.four.at[int(upper)], self.torus.near(by, 0))

    def swap(self, split):
        self.arrive(30, self.four.at[0])
        self.arrive(31, self.four.at[1])
        self.add(self.view(0, 0), self.four.at[0], self.four.at[1])
        low, high = split(self.total[self.chip(0, 0)].astype(F32))
        core = self.torus.core
        self.kinds[core] = jnp.where(core == 0, low, high).astype(BF16)
        self.leave[...] = jnp.where(core == 0, high, low).astype(BF16)
        self.send(48, self.leave, self.kinds.at[core], self.sibling)

    def cross(self):
        kind = self.torus.row // 2
        self.arrive(48, self.kinds.at[1 - self.torus.core])
        self.send(49, self.kinds.at[1 - kind], self.row_in.at[0], self.torus.across)

    def pair_up(self, out):
        kind = self.torus.row // 2
        self.arrive(49, self.row_in.at[0])
        value = self.kinds[kind].astype(F32) + self.row_in[0].astype(F32)
        out[...] = value
        self.row_in[1] = value.astype(BF16)
        self.send(50, self.row_in.at[1], self.row_in.at[2], self.torus.beside)

    def end(self, out):
        self.arrive(50, self.row_in.at[2])
        out[...] += self.row_in[2].astype(F32)


class Exchange(Lane):
    def __init__(self, base, send_sem, recv_sem, torus, sums, incoming):
        super().__init__(base, send_sem, recv_sem, torus.sibling)
        self.torus, self.sums, self.incoming = torus, sums, incoming
        turn_y, turn_z = 1 - 2 * (torus.y % 2), 1 - 2 * (torus.z % 2)
        first = jnp.where(torus.core == 0, turn_y, turn_z)
        second = jnp.where(torus.core == 0, turn_z, turn_y)
        self.partners = [torus.near(first, 0), torus.near(-first, 0)]
        self.partners += [torus.near(0, second), torus.near(0, -second), torus.beside, torus.across]
        self.done = 0

    def begin(self, parts):
        core = self.torus.core
        self.send(6, parts.at[1 - core], self.incoming.at[6], self.sibling)
        self.arrive(6, self.incoming.at[6])
        self.sums[0] = parts[core] + self.incoming[6]
        self.start()

    def start(self):
        k = self.done
        self.send(k, self.sums.at[k], self.incoming.at[k], self.partners[k])

    def step(self):
        k = self.done
        self.arrive(k, self.incoming.at[k])
        self.sums[k + 1] = self.sums[k] + self.incoming[k]
        self.done += 1
        if self.done < 6:
            self.start()
        else:
            self.send(7, self.sums.at[6], self.incoming.at[7], self.sibling)

    def end(self, out):
        self.arrive(7, self.incoming.at[7])
        own = self.torus.row // 2 == self.torus.core
        out[...] = jnp.where(own, self.sums[6], self.incoming[7])


def layer_kernel(
    kind_ref, rank_ref, x_ref, cot_ref, q_in, o_in, gain_in,
    enc_ref, grad_ref, out_q, out_o, out_gain,
    wq, wp, wo, gain_s, sib_q, sib_o, sib_gain, xhat_s, inv_s, qkv_s, dattn_s, mixed_s, dqkv_s, ht_s, mt_s,
    dx_s, dgain_s, gain_sums, gain_rows, give_q, give_o, total_q, total_o, *rest,
):
    held_q, held_o = rest[0:16:2], rest[1:16:2]
    gather_send, gather_recv, scatter_send, scatter_recv, gain_send, gain_recv = rest[16:]
    blocks, window, width = x_ref.shape
    inner = wo.shape[1]
    rows = inner // CHIPS
    share = width // CHIPS
    padded = wp.shape[2]
    torus = Torus()
    torus.meet()
    core = torus.core
    first = core == 0

    early = Lane(2 * 48, gather_send, gather_recv, torus.sibling)
    early.send(0, o_in.at[1 - core], sib_o, torus.sibling)
    early.send(1, gain_in.at[1 - core], sib_gain, torus.sibling)
    early.send(2, q_in.at[1 - core], sib_q, torus.sibling)
    pending = []
    gather_o = Gather(0, gather_send, gather_recv, torus, wp, AWAY_O, pending)
    gather_q = Gather(48, gather_send, gather_recv, torus, wq, AWAY_Q, pending)
    gathers = (gather_o, gather_q)
    here = torus.y * RING + torus.z
    early.arrive(0, sib_o)
    early.arrive(1, sib_gain)
    mine, other = o_in[core].astype(F32), sib_o[...].astype(F32)
    gain_row = gain_in[core] + sib_gain[...]
    wp[core, here] = jnp.concatenate(
        [
            jnp.where(first, mine, other),
            jnp.where(first, other, mine),
            gain_row,
            jnp.zeros((padded - 2 * mine.shape[0] - 1, width), F32),
        ],
        axis=0,
    ).astype(BF16)
    gather_o.begin()
    early.arrive(2, sib_q)
    mine, other = q_in[core].astype(F32), sib_q[...].astype(F32)
    wq[core, here] = jnp.concatenate(
        [jnp.where(first, mine, other), jnp.where(first, other, mine)], axis=0
    ).astype(BF16)
    gather_q.begin()

    def norm_block(b):
        x_hat, inverse = normalized(x_ref[b].astype(F32))
        xhat_s[b] = x_hat
        inv_s[b] = jnp.broadcast_to(inverse, inv_s.shape[1:])

    norm_block(0)
    for one in gathers:
        one.ring_back()
        one.ring_ahead()
    norm_block(1)
    gather_o.second_near(0)
    gather_o.ring_far()
    gather_q.second_near(0)
    norm_block(2)
    gather_o.second_near(1)
    gather_o.second_near(2)
    gather_o.second_far(0)
    gather_q.ring_far()
    norm_block(3)
    gather_o.second_near(3)
    gather_o.second_far(1)
    gather_o.second_far(2)
    gather_q.second_near(1)
    gather_q.second_near(2)
    gather_q.second_far(0)
    gather_o.second_far(3)
    gather_q.second_near(3)
    gather_q.second_far(1)
    gather_q.second_far(2)
    gather_q.second_far(3)
    for one, n, j in pending:
        one.complete(n, j)
    gather_o.other_kind()

    @pl.loop(0, 2)
    def _(m):
        for chip in range(0, CHIPS, 2):
            two = [wp[m, chip + i, 0:rows].astype(F32) for i in range(2)]
            wo[m, chip * rows : (chip + 2) * rows] = jnp.concatenate(two, axis=0).astype(BF16)
        gain_s[m] = sum(wp[m, chip, rows : rows + 1].astype(F32) for chip in range(CHIPS))

    def weights(kind, low, high):
        return wq[kind, :, :, low:high].reshape(width, high - low)

    @pl.loop(0, blocks)
    def _(b):
        kind = kind_ref[b]
        columns = pl.ds(pl.multiple_of(b * WIN, WIN), WIN)
        turned = (xhat_s[b] * gain_s[kind]).astype(BF16).T
        for m in range(2):
            ht_s[m, :, columns] = jnp.where(kind == m, turned, jnp.zeros_like(turned))
        dattn_s[b] = nt_dot(cot_ref[b], wo[kind]).astype(BF16)

    gather_q.other_kind()

    @pl.loop(0, blocks)
    def _(b):
        kind = kind_ref[b]
        columns = pl.ds(pl.multiple_of(b * WIN, WIN), WIN)
        normed = (xhat_s[b] * gain_s[kind]).astype(BF16)
        for at in range(0, 3 * inner, inner):
            qkv_s[:, at : at + inner] = nn_dot(normed, weights(kind, at, at + inner)).astype(BF16)
        attend_block(kind == 0, qkv_s, dattn_s.at[b], mixed_s.at[b], dqkv_s.at[b])
        mixed_t = mixed_s[b].T
        for m in range(2):
            mt_s[m, :, columns] = jnp.where(kind == m, mixed_t, jnp.zeros_like(mixed_t))

    scatter_q = Scatter(
        0, scatter_send, scatter_recv, torus, give_q, total_q, held_q, AWAY_Q
    )
    scatter_o = Scatter(
        STEPS, scatter_send, scatter_recv, torus, give_o, total_o, held_o, AWAY_O
    )
    tokens = blocks * window
    d_qkv_all = dqkv_s[...].reshape(tokens, 3 * inner)

    def q_block(kind, j):
        parts = []
        for n in range(4):
            chip = torus.chip(OFFSETS[n], OFFSETS[j], kind)
            at = pl.ds(pl.multiple_of(chip * share, 16), share)
            parts.append(ht_s[kind, at, :])
        return nn_dot(jnp.concatenate(parts, axis=0), d_qkv_all)

    cot_all = cot_ref[...].reshape(tokens, width)

    def o_rows(kind, store):
        below = jnp.zeros((padded - rows, width), F32)
        for at in range(0, CHIPS, 4):
            four = nn_dot(mt_s[kind, at * rows : (at + 4) * rows, :], cot_all)
            for i in range(4):
                store(at + i, jnp.concatenate([four[i * rows : (i + 1) * rows], below], axis=0))

    def store_given(chip, value):
        give_o[chip] = value.astype(BF16)

    o_rows(1 - core, store_given)
    for j in (3, 2, 1, 0):
        scatter_o.give(j)
    for j in (3, 2, 1, 0):
        found = q_block(1 - core, j)
        for n in range(4):
            chip = torus.chip(OFFSETS[n], OFFSETS[j], 1 - core)
            give_q[chip] = found[n * share : (n + 1) * share].astype(BF16)
        scatter_q.give(j)

    def take_q(j):
        found = q_block(core, j)
        scatter_q.take(j, lambda n, chip: found[n * share : (n + 1) * share])

    gather_o.finish()

    def keep_own(chip, value):
        wp[core, chip] = value.astype(BF16)

    o_rows(core, keep_own)

    def take_o(j):
        scatter_o.take(j, lambda n, chip: wp[core, chip].astype(F32))

    take_q(3)
    take_q(2)
    take_o(3)
    take_o(2)
    scatter_q.take_lent(3)
    scatter_q.send_far()
    scatter_o.take_lent(3)
    scatter_o.send_far()
    take_q(1)
    scatter_q.take_lent(2)
    scatter_q.send_near(2)
    scatter_q.take_lent(1)
    scatter_q.send_near(1)
    take_q(0)
    take_o(1)
    take_o(0)
    scatter_o.take_lent(2)
    scatter_o.send_near(2)
    scatter_o.take_lent(1)
    scatter_o.send_near(1)
    dgain_s[...] = jnp.zeros_like(dgain_s)

    def finish_blocks(low, high):
        @pl.loop(low, high)
        def _(b):
            kind = kind_ref[b]
            x_hat = xhat_s[b]
            gain = gain_s[kind]
            y = x_ref[b].astype(F32) + nn_dot(mixed_s[b], wo[kind])
            d_normed = nt_dot(dqkv_s[b], weights(kind, 0, 3 * inner))
            d_gain = jnp.sum(d_normed * x_hat, axis=0, keepdims=True)
            for m in range(2):
                dgain_s[m] += jnp.where(kind == m, d_gain, jnp.zeros_like(d_gain))
            scaled = d_normed * gain
            d_input = inv_s[b][:, 0:1] * (
                scaled
                - jnp.mean(scaled, axis=-1, keepdims=True)
                - x_hat * jnp.mean(scaled * x_hat, axis=-1, keepdims=True)
            )
            dx_s[b] = (cot_ref[b].astype(F32) + d_input).astype(BF16)
            xhat_s[b] = y

    finish_blocks(0, blocks)
    gains = Exchange(0, gain_send, gain_recv, torus, gain_sums, gain_rows)
    gains.begin(dgain_s)
    scatter_q.take_lent(0)
    scatter_q.first_far()
    gains.step()
    scatter_o.take_lent(0)
    scatter_o.first_far()
    gains.step()
    scatter_q.first_near()
    gains.step()
    for r in range(blocks):
        y, dx = xhat_s[0], dx_s[0]
        for b in range(1, blocks):
            y = jnp.where(rank_ref[b] == r, xhat_s[b], y)
            dx = jnp.where(rank_ref[b] == r, dx_s[b], dx)
        enc_ref[r] = y.astype(BF16)
        grad_ref[r] = dx
    scatter_o.first_near()
    gains.step()
    scatter_q.swap(lambda value: (value[: share // 2], value[share // 2 :]))
    gains.step()
    def split_o(value):
        half = rows // 2
        below = jnp.concatenate([value[rows : rows + 1], jnp.zeros((3, width), F32)], axis=0)
        return (
            jnp.concatenate([value[:half], below], axis=0),
            jnp.concatenate([value[half:rows], below], axis=0),
        )

    scatter_o.swap(split_o)
    scatter_q.cross()
    gains.step()
    scatter_o.cross()
    scatter_q.pair_up(out_q)
    scatter_o.pair_up(out_o)
    gains.end(out_gain)
    scatter_q.end(out_q)
    scatter_o.end(out_o)
    for one in (early, gather_o, gather_q, scatter_q, scatter_o, gains):
        one.finish()


def layer(kind, rank, blocks, cotangent, qkv_weight, out_weight, gain_row):
    count, window, width = blocks.shape
    inner = qkv_weight.shape[2] // 3
    tokens = count * window
    rows = inner // CHIPS
    padded = -(-(rows + 1) // 16) * 16
    q, o = (width // CHIPS, 3 * inner), (padded, width)
    half_q, half_o = qkv_weight.shape[1:], (-(-(rows // 2 + 1) // 8) * 8, width)
    scratch = [
        pltpu.VMEM((2, CHIPS) + q, BF16),
        pltpu.VMEM((2, CHIPS) + o, BF16),
        pltpu.VMEM((2, inner, width), BF16),
        pltpu.VMEM((2, 1, width), F32),
        pltpu.VMEM(qkv_weight.shape[1:], BF16),
        pltpu.VMEM(out_weight.shape[1:], BF16),
        pltpu.VMEM((1, width), F32),
        pltpu.VMEM((count, window, width), F32),
        pltpu.VMEM((count, window, LANES), F32),
        pltpu.VMEM((window, 3 * inner), BF16),
        pltpu.VMEM((count, window, inner), BF16),
        pltpu.VMEM((count, window, inner), BF16),
        pltpu.VMEM((count, window, 3 * inner), BF16),
        pltpu.VMEM((2, width, tokens), BF16),
        pltpu.VMEM((2, inner, tokens), BF16),
        pltpu.VMEM((count, window, width), BF16),
        pltpu.VMEM((2, 1, width), F32),
        pltpu.VMEM((7, 1, width), F32),
        pltpu.VMEM((8, 1, width), F32),
        pltpu.VMEM((CHIPS,) + q, BF16),
        pltpu.VMEM((CHIPS,) + o, BF16),
        pltpu.VMEM((CHIPS,) + q, BF16),
        pltpu.VMEM((CHIPS,) + o, BF16),
    ]
    for lead in ((4,), (4, 2), (), (2,)):
        scratch += [
            pltpu.VMEM(lead + (q[0], q[1] - AWAY_Q), BF16),
            pltpu.VMEM(lead + (o[0], o[1] - AWAY_O), BF16),
        ]
    scratch += [
        pltpu.VMEM((CHIPS, q[0], AWAY_Q), BF16),
        pltpu.VMEM((CHIPS, o[0], AWAY_O), BF16),
    ]
    for lead in ((2,), (), (3,)):
        scratch += [pltpu.VMEM(lead + half_q, BF16), pltpu.VMEM(lead + half_o, BF16)]
    scratch += [pltpu.SemaphoreType.DMA((2 * 48 + 3,))] * 2
    scratch += [pltpu.SemaphoreType.DMA((2 * STEPS,))] * 2
    scratch += [pltpu.SemaphoreType.DMA((8,))] * 2
    vmem = pl.BlockSpec(memory_space=pltpu.VMEM)
    return pl.pallas_call(
        layer_kernel,
        out_shape=(
            jax.ShapeDtypeStruct(blocks.shape, BF16),
            jax.ShapeDtypeStruct(blocks.shape, BF16),
            jax.ShapeDtypeStruct(half_q, F32),
            jax.ShapeDtypeStruct(half_o, F32),
            jax.ShapeDtypeStruct((1, width), F32),
        ),
        in_specs=[pl.BlockSpec(memory_space=pltpu.SMEM)] * 2 + [vmem] * 5,
        out_specs=(vmem,) * 5,
        scratch_shapes=scratch,
        compiler_params=pltpu.CompilerParams(
            collective_id=0, has_side_effects=True, vmem_limit_bytes=VMEM_BYTES
        ),
    )(kind, rank, blocks, cotangent, qkv_weight, out_weight, gain_row)


def shards(blocks, cotangent, modality, time_rank, qkv_weight, out_weight, norm_gain):
    rows, width = out_weight.shape[1:]
    share = norm_gain.shape[1]
    start = lax.axis_index("dp") * share
    gain_row = lax.dynamic_update_slice(
        jnp.zeros((2, width), F32), norm_gain.astype(F32), (0, start)
    )[:, None, :]
    encoded, block_grad, share_qkv, share_packed, gains = layer(
        modality, time_rank, blocks, cotangent, qkv_weight, out_weight, gain_row
    )
    share_gain = lax.dynamic_slice(gains, (0, start), (1, share))
    return (encoded, block_grad, share_qkv[None], share_packed[None, :rows], share_gain)


def solution(mesh):
    return jax.shard_map(
        shards,
        mesh=mesh,
        in_specs=(
            P(("grp", "dp"), None, None),
            P(("grp", "dp"), None, None),
            P(("grp", "dp")),
            P(("grp", "dp")),
            P(None, "dp", None),
            P(None, "dp", None),
            P(None, "dp"),
        ),
        out_specs=(
            P(("grp", "dp"), None, None),
            P(("grp", "dp"), None, None),
            P("grp", "dp", None),
            P("grp", "dp", None),
            P("grp", "dp"),
        ),
        check_vma=False,
    )
```

```python
import math

import jax
import jax.numpy as jnp
from jax import lax
from jax.experimental import pallas as pl
from jax.experimental.pallas import tpu as pltpu
from jax.sharding import PartitionSpec as P

A_HEADS = 10
A_SIZE = 64
V_HEADS = 8
V_SIZE = 80
WIN = 128
VWIN = 64
LANES = 128
EPSILON = 1e-05
VMEM_BYTES = 62 * 1024 * 1024
RING = 4
CHIPS = RING * RING
STEPS = 51
BEHIND = 6
AWAY_Q, AWAY_O = 5 * LANES, 3 * LANES
MESH = pl.DeviceIdType.MESH
OFFSETS = (0, -1, 1, 2)
UP = (True, False, False, True)
BF16, F32 = jnp.bfloat16, jnp.float32


def normalized(x):
    mean_row = jnp.mean(x, axis=-1, keepdims=True)
    centered = x - mean_row
    inverse = lax.rsqrt(jnp.mean(centered * centered, axis=-1, keepdims=True) + EPSILON)
    return centered * inverse, inverse


def nt_dot(a, b):
    return lax.dot_general(a, b, (((1,), (1,)), ((), ())), preferred_element_type=F32)


def tn_dot(a, b):
    return lax.dot_general(a, b, (((0,), (0,)), ((), ())), preferred_element_type=F32)


def nn_dot(a, b):
    return jnp.dot(a, b, preferred_element_type=F32)


def attend_pair(query, keys, values, cot, first, second, scale, same_window):
    zero = jnp.zeros((), BF16)

    def stacked(rows):
        return jnp.concatenate(
            [jnp.where(first, rows, zero), jnp.where(second, rows, zero)], axis=0
        )

    query_two = stacked(query)
    cot_two = stacked(cot)
    scores = jnp.where(same_window, nt_dot(query_two, keys) * scale, -1e30)
    row_max = jnp.max(scores, axis=-1, keepdims=True)
    exponent = jnp.exp(scores - row_max)
    probs = exponent * (1.0 / jnp.sum(exponent, axis=-1, keepdims=True))
    probs_low = probs.astype(BF16)
    d_probs = nt_dot(cot_two, values)
    inner = jnp.sum(d_probs * probs, axis=-1, keepdims=True)
    d_scores = (probs * (d_probs - inner) * scale).astype(BF16)

    def beside(rows):
        return jnp.concatenate([rows[:WIN], rows[WIN:]], axis=1)

    mixed = nn_dot(beside(probs_low), stacked(values))
    d_values = tn_dot(probs_low, cot_two)
    d_query = nn_dot(beside(d_scores), stacked(keys))
    d_keys = tn_dot(d_scores, query_two)
    return mixed, d_query, d_keys, d_values


def attend_block(audio, qkv, cot, out, d_qkv):
    inner = cot.shape[1]
    tile_count = inner // LANES
    scale = jnp.where(audio, 1.0 / math.sqrt(A_SIZE), 1.0 / math.sqrt(V_SIZE)).astype(F32)
    size = jnp.where(audio, A_SIZE, V_SIZE)
    row = lax.broadcasted_iota(jnp.int32, (2 * WIN, WIN), 0)
    col = lax.broadcasted_iota(jnp.int32, (2 * WIN, WIN), 1)
    apart = ((row % WIN) // VWIN != col // VWIN).astype(jnp.int32)
    same_window = apart * jnp.where(audio, 0, 1) == 0
    tiles = [[None] * tile_count for _ in range(4)]
    for pair in range(A_HEADS // 2):
        start, stop = pair * LANES, min((pair + 2) * LANES, inner)
        low = jnp.where(audio, 2 * pair * A_SIZE, 2 * pair * V_SIZE)
        lane = lax.broadcasted_iota(jnp.int32, (WIN, stop - start), 1) + start
        first = (lane >= low) & (lane < low + size)
        second = (lane >= low + size) & (lane < low + 2 * size)
        found = attend_pair(
            qkv[:, start:stop],
            qkv[:, inner + start : inner + stop],
            qkv[:, 2 * inner + start : 2 * inner + stop],
            cot[:, start:stop],
            first,
            second,
            scale,
            same_window,
        )
        for which in range(4):
            for tile in range(start // LANES, stop // LANES):
                at = tile * LANES - start
                part = found[which][:, at : at + LANES]
                held = tiles[which][tile]
                tiles[which][tile] = part if held is None else held + part
        at = slice(start, start + LANES)
        out[:, at] = tiles[0][pair].astype(BF16)
        for which in range(3):
            to = slice(which * inner + start, which * inner + start + LANES)
            d_qkv[:, to] = tiles[which + 1][pair].astype(BF16)


def step_on(position, by):
    return lax.rem(position + by + RING, RING)


class Torus:
    def __init__(self):
        self.row = lax.axis_index("grp")
        self.index = lax.axis_index("dp")
        self.core = self.index % 2
        self.y, self.z = self.index // (2 * RING), self.index // 2 % RING

    def chip(self, first_by, second_by, kind):
        y_by = jnp.where(kind == 0, first_by, second_by)
        z_by = jnp.where(kind == 0, second_by, first_by)
        return step_on(self.y, y_by) * RING + step_on(self.z, z_by)

    def near(self, first_by, second_by):
        return (self.row, self.chip(first_by, second_by, self.core) * 2 + self.core)

    def meet(self):
        self.sibling = (self.row, self.index + 1 - 2 * self.core)
        self.across = (RING - 1 - self.row, self.index)
        self.beside = (self.row + 1 - 2 * (self.row % 2), self.index)
        peers = [self.near(1, 0), self.near(-1, 0), self.near(0, 1), self.near(0, -1)]
        peers += [self.sibling, self.across, self.beside]
        barrier = pltpu.get_barrier_semaphore()
        for peer in peers:
            pl.semaphore_signal(barrier, inc=1, device_id=peer, device_id_type=MESH)
        pl.semaphore_wait(barrier, len(peers))


class Lane:
    def __init__(self, base, send_sem, recv_sem, sibling):
        self.base, self.send_sem, self.recv_sem = base, send_sem, recv_sem
        self.sibling = sibling
        self.sent = []

    def copy(self, number, source, target, device):
        return pltpu.make_async_remote_copy(
            src_ref=source,
            dst_ref=target,
            send_sem=self.send_sem.at[self.base + number],
            recv_sem=self.recv_sem.at[self.base + number],
            device_id=device,
            device_id_type=MESH,
        )

    def send(self, number, source, target, device):
        made = self.copy(number, source, target, device)
        made.start()
        self.sent.append(made)

    def arrive(self, number, target):
        self.copy(number, target, target, self.sibling).wait_recv()

    def finish(self):
        for made in self.sent:
            made.wait_send()
        self.sent = []


class Slots(Lane):
    def __init__(self, base, send_sem, recv_sem, torus, columns, away):
        super().__init__(base, send_sem, recv_sem, torus.sibling)
        self.torus, self.away, self.carried = torus, away, columns - away
        odd = torus.row % 2
        self.start = pl.multiple_of(away * (1 - odd), LANES)
        self.missing = pl.ds(pl.multiple_of(self.carried * odd, LANES), away)
        self.lent = pl.ds(pl.multiple_of(self.carried * (1 - odd), LANES), away)
        self.cut = -(-self.carried // (2 * LANES)) * LANES

    def chip(self, n, j):
        return self.torus.chip(OFFSETS[n], OFFSETS[j], self.torus.core)

    def window(self):
        return pl.ds(self.start, self.carried)

    def half_window(self, upper):
        if upper:
            return pl.ds(self.start + self.cut, self.carried - self.cut)
        return pl.ds(self.start, self.cut)

    def neighbour(self, n, j):
        return self.torus.across if (n + j) % 2 else self.torus.beside


class Gather(Slots):
    def __init__(self, base, send_sem, recv_sem, torus, held, away, pending):
        super().__init__(base, send_sem, recv_sem, torus, held.shape[-1], away)
        self.held, self.pending = held, pending

    def slot(self, n, j, columns=None):
        columns = self.window() if columns is None else columns
        return self.held.at[self.torus.core, self.chip(n, j), :, columns]

    def half(self, n, upper):
        return self.slot(n, 0, self.half_window(upper))

    def pass_on(self, number, view, first_by, second_by):
        self.send(number, view, view, self.torus.near(first_by, second_by))

    def share(self, n, j):
        view = self.held.at[self.torus.core, self.chip(n, j)]
        self.send(16 + 4 * n + j, view, view, self.sibling)

    def lend(self, n, j):
        view = self.slot(n, j, self.lent)
        self.send(32 + 4 * n + j, view, view, self.neighbour(n, j))
        self.pending.append((self, n, j))
        if len(self.pending) > BEHIND:
            one, n, j = self.pending.pop(0)
            one.complete(n, j)

    def complete(self, n, j):
        self.arrive(32 + 4 * n + j, self.slot(n, j, self.missing))
        self.share(n, j)

    def along_second(self, n):
        self.pass_on(4 + 2 * n, self.slot(n, 0), 0, 1)
        self.pass_on(5 + 2 * n, self.slot(n, 0), 0, -1)

    def begin(self):
        self.pass_on(0, self.slot(0, 0), 1, 0)
        self.pass_on(1, self.slot(0, 0), -1, 0)
        self.along_second(0)
        self.share(0, 0)

    def ring_back(self):
        self.arrive(0, self.slot(1, 0))
        self.pass_on(2, self.half(1, False), 1, 0)
        self.along_second(1)
        self.lend(1, 0)

    def ring_ahead(self):
        self.arrive(1, self.slot(2, 0))
        self.pass_on(3, self.half(2, True), -1, 0)
        self.along_second(2)
        self.lend(2, 0)

    def ring_far(self):
        self.arrive(2, self.half(3, False))
        self.arrive(3, self.half(3, True))
        self.along_second(3)
        self.lend(3, 0)

    def second_near(self, n):
        self.arrive(4 + 2 * n, self.slot(n, 1))
        if UP[n]:
            self.pass_on(12 + n, self.slot(n, 1), 0, 1)
        self.lend(n, 1)
        self.arrive(5 + 2 * n, self.slot(n, 2))
        if not UP[n]:
            self.pass_on(12 + n, self.slot(n, 2), 0, -1)
        self.lend(n, 2)

    def second_far(self, n):
        self.arrive(12 + n, self.slot(n, 3))
        self.lend(n, 3)

    def other_kind(self):
        other = 1 - self.torus.core
        for j in range(4):
            for n in range(4):
                chip = self.torus.chip(OFFSETS[n], OFFSETS[j], other)
                self.arrive(16 + 4 * n + j, self.held.at[other, chip])


class Scatter(Slots):
    def __init__(self, base, send_sem, recv_sem, torus, given, total, held, away):
        super().__init__(base, send_sem, recv_sem, torus, total.shape[-1], away)
        self.given, self.total = given, total
        self.one, self.two, self.three, self.four, self.lent_in = held[:5]
        self.kinds, self.leave, self.row_in = held[5:]

    def view(self, n, j, columns=None):
        columns = self.window() if columns is None else columns
        return self.total.at[self.chip(n, j), :, columns]

    def part(self, upper):
        return self.three.at[:, slice(self.cut, None) if upper else slice(0, self.cut)]

    def add(self, target, *terms):
        value = target[...].astype(F32)
        for term in terms:
            value = value + term[...].astype(F32)
        target[...] = value.astype(BF16)

    def give(self, j):
        for n in range(4):
            chip = self.torus.chip(OFFSETS[n], OFFSETS[j], 1 - self.torus.core)
            self.send(4 * j + n, self.given.at[chip], self.total.at[chip], self.sibling)

    def take(self, j, own):
        for n in range(4):
            chip = self.chip(n, j)
            self.arrive(4 * j + n, self.total.at[chip])
            value = own(n, chip) + self.total[chip].astype(F32)
            self.total[chip] = value.astype(BF16)
            if n or j:
                lent = self.view(n, j, self.missing)
                self.send(32 + 4 * j + n, lent, self.lent_in.at[4 * j + n], self.neighbour(n, j))

    def take_lent(self, j):
        for n in range(4):
            if n or j:
                self.arrive(32 + 4 * j + n, self.lent_in.at[4 * j + n])
                self.add(self.view(n, j, self.lent), self.lent_in.at[4 * j + n])

    def send_far(self):
        for n in range(4):
            device = self.torus.near(0, 1 if UP[n] else -1)
            self.send(16 + n, self.view(n, 3), self.one.at[n], device)

    def send_near(self, j):
        for n in (3, 1, 2, 0):
            if UP[n] == (j == 2):
                self.arrive(16 + n, self.one.at[n])
                self.add(self.view(n, j), self.one.at[n])
            number, which = (20 + 2 * n, 0) if j == 2 else (21 + 2 * n, 1)
            device = self.torus.near(0, OFFSETS[j])
            self.send(number, self.view(n, j), self.two.at[n, which], device)

    def close_second(self, n):
        self.arrive(20 + 2 * n, self.two.at[n, 0])
        self.arrive(21 + 2 * n, self.two.at[n, 1])
        self.add(self.view(n, 0), self.two.at[n, 0], self.two.at[n, 1])

    def first_far(self):
        self.close_second(3)
        for upper, by in ((False, 1), (True, -1)):
            view = self.view(3, 0, self.half_window(upper))
            self.send(28 + upper, view, self.part(upper), self.torus.near(by, 0))
        for n in (2, 1, 0):
            self.close_second(n)

    def first_near(self):
        for n, upper, by in ((2, False, 1), (1, True, -1)):
            self.arrive(28 + upper, self.part(upper))
            self.add(self.view(n, 0, self.half_window(upper)), self.part(upper))
            self.send(30 + upper, self.view(n, 0), self.four.at[int(upper)], self.torus.near(by, 0))

    def swap(self, split):
        self.arrive(30, self.four.at[0])
        self.arrive(31, self.four.at[1])
        self.add(self.view(0, 0), self.four.at[0], self.four.at[1])
        low, high = split(self.total[self.chip(0, 0)].astype(F32))
        core = self.torus.core
        self.kinds[core] = jnp.where(core == 0, low, high).astype(BF16)
        self.leave[...] = jnp.where(core == 0, high, low).astype(BF16)
        self.send(48, self.leave, self.kinds.at[core], self.sibling)

    def cross(self):
        kind = self.torus.row // 2
        self.arrive(48, self.kinds.at[1 - self.torus.core])
        self.send(49, self.kinds.at[1 - kind], self.row_in.at[0], self.torus.across)

    def pair_up(self, out):
        kind = self.torus.row // 2
        self.arrive(49, self.row_in.at[0])
        value = self.kinds[kind].astype(F32) + self.row_in[0].astype(F32)
        out[...] = value
        self.row_in[1] = value.astype(BF16)
        self.send(50, self.row_in.at[1], self.row_in.at[2], self.torus.beside)

    def end(self, out):
        self.arrive(50, self.row_in.at[2])
        out[...] += self.row_in[2].astype(F32)


def layer_kernel(
    kind_ref, rank_ref, x_ref, cot_ref, q_in, o_in, gain_in,
    enc_ref, grad_ref, out_q, out_o,
    wq, wp, wo, gain_s, sib_q, sib_o, sib_gain, xhat_s, inv_s, qkv_s, dattn_s, mixed_s, dqkv_s, ht_s, mt_s,
    y_s, dx_s, dgain_s, give_q, give_o, total_q, total_o, *rest,
):
    held_q, held_o = rest[0:16:2], rest[1:16:2]
    gather_send, gather_recv, scatter_send, scatter_recv = rest[16:]
    blocks, window, width = x_ref.shape
    inner = wo.shape[1]
    rows = inner // CHIPS
    share = width // CHIPS
    padded = wp.shape[2]
    torus = Torus()
    torus.meet()
    core = torus.core
    first = core == 0

    early = Lane(2 * 48, gather_send, gather_recv, torus.sibling)
    early.send(0, o_in.at[1 - core], sib_o, torus.sibling)
    early.send(1, gain_in.at[1 - core], sib_gain, torus.sibling)
    early.send(2, q_in.at[1 - core], sib_q, torus.sibling)
    pending = []
    gather_o = Gather(0, gather_send, gather_recv, torus, wp, AWAY_O, pending)
    gather_q = Gather(48, gather_send, gather_recv, torus, wq, AWAY_Q, pending)
    gathers = (gather_o, gather_q)
    here = torus.y * RING + torus.z
    early.arrive(0, sib_o)
    early.arrive(1, sib_gain)
    mine, other = o_in[core].astype(F32), sib_o[...].astype(F32)
    gain_row = gain_in[core] + sib_gain[...]
    wp[core, here] = jnp.concatenate(
        [
            jnp.where(first, mine, other),
            jnp.where(first, other, mine),
            gain_row,
            jnp.zeros((padded - 2 * mine.shape[0] - 1, width), F32),
        ],
        axis=0,
    ).astype(BF16)
    gather_o.begin()
    early.arrive(2, sib_q)
    mine, other = q_in[core].astype(F32), sib_q[...].astype(F32)
    wq[core, here] = jnp.concatenate(
        [jnp.where(first, mine, other), jnp.where(first, other, mine)], axis=0
    ).astype(BF16)
    gather_q.begin()

    def norm_block(b):
        x_hat, inverse = normalized(x_ref[b].astype(F32))
        xhat_s[b] = x_hat
        inv_s[b] = jnp.broadcast_to(inverse, inv_s.shape[1:])

    norm_block(0)
    for one in gathers:
        one.ring_back()
        one.ring_ahead()
    norm_block(1)
    for one in gathers:
        one.second_near(0)
    norm_block(2)
    for one in gathers:
        one.ring_far()
    norm_block(3)
    for one in gathers:
        one.second_near(1)
        one.second_near(2)
        one.second_far(0)
    for one in gathers:
        one.second_near(3)
        one.second_far(1)
        one.second_far(2)
        one.second_far(3)
    for one, n, j in pending:
        one.complete(n, j)
    gather_o.other_kind()

    @pl.loop(0, 2)
    def _(m):
        for chip in range(0, CHIPS, 2):
            two = [wp[m, chip + i, 0:rows].astype(F32) for i in range(2)]
            wo[m, chip * rows : (chip + 2) * rows] = jnp.concatenate(two, axis=0).astype(BF16)
        gain_s[m] = sum(wp[m, chip, rows : rows + 1].astype(F32) for chip in range(CHIPS))

    gather_q.other_kind()

    def weights(kind, low, high):
        return wq[kind, :, :, low:high].reshape(width, high - low)

    @pl.loop(0, blocks)
    def _(b):
        kind = kind_ref[b]
        normed = (xhat_s[b] * gain_s[kind]).astype(BF16)
        columns = pl.ds(pl.multiple_of(b * WIN, WIN), WIN)
        turned = normed.T
        for m in range(2):
            ht_s[m, :, columns] = jnp.where(kind == m, turned, jnp.zeros_like(turned))
        for at in range(0, 3 * inner, inner):
            qkv_s[:, at : at + inner] = nn_dot(normed, weights(kind, at, at + inner)).astype(BF16)
        dattn_s[...] = nt_dot(cot_ref[b], wo[kind]).astype(BF16)
        attend_block(kind == 0, qkv_s, dattn_s, mixed_s.at[b], dqkv_s.at[b])
        mixed_t = mixed_s[b].T
        for m in range(2):
            mt_s[m, :, columns] = jnp.where(kind == m, mixed_t, jnp.zeros_like(mixed_t))

    scatter_q = Scatter(
        0, scatter_send, scatter_recv, torus, give_q, total_q, held_q, AWAY_Q
    )
    scatter_o = Scatter(
        STEPS, scatter_send, scatter_recv, torus, give_o, total_o, held_o, AWAY_O
    )
    tokens = blocks * window
    d_qkv_all = dqkv_s[...].reshape(tokens, 3 * inner)

    def q_block(kind, j):
        parts = []
        for n in range(4):
            chip = torus.chip(OFFSETS[n], OFFSETS[j], kind)
            at = pl.ds(pl.multiple_of(chip * share, 16), share)
            parts.append(ht_s[kind, at, :])
        return nn_dot(jnp.concatenate(parts, axis=0), d_qkv_all)

    for j in (3, 2, 1, 0):
        found = q_block(1 - core, j)
        for n in range(4):
            chip = torus.chip(OFFSETS[n], OFFSETS[j], 1 - core)
            give_q[chip] = found[n * share : (n + 1) * share].astype(BF16)
        scatter_q.give(j)

    def take_q(j):
        found = q_block(core, j)
        scatter_q.take(j, lambda n, chip: found[n * share : (n + 1) * share])

    take_q(3)
    take_q(2)
    scatter_q.take_lent(3)
    scatter_q.send_far()
    take_q(1)
    scatter_q.take_lent(2)
    scatter_q.send_near(2)
    scatter_q.take_lent(1)
    scatter_q.send_near(1)
    take_q(0)
    dgain_s[...] = jnp.zeros_like(dgain_s)

    def finish_blocks(low, high):
        @pl.loop(low, high)
        def _(b):
            kind = kind_ref[b]
            x_hat = xhat_s[b]
            gain = gain_s[kind]
            y = x_ref[b].astype(F32) + nn_dot(mixed_s[b], wo[kind])
            y_s[b] = y.astype(BF16)
            d_normed = nt_dot(dqkv_s[b], weights(kind, 0, 3 * inner))
            d_gain = jnp.sum(d_normed * x_hat, axis=0, keepdims=True)
            for m in range(2):
                dgain_s[m] += jnp.where(kind == m, d_gain, jnp.zeros_like(d_gain))
            scaled = d_normed * gain
            d_input = inv_s[b][:, 0:1] * (
                scaled
                - jnp.mean(scaled, axis=-1, keepdims=True)
                - x_hat * jnp.mean(scaled * x_hat, axis=-1, keepdims=True)
            )
            dx_s[b] = (cot_ref[b].astype(F32) + d_input).astype(BF16)

    finish_blocks(0, blocks)
    cot_all = cot_ref[...].reshape(tokens, width)

    def o_rows(kind, store):
        below = jnp.concatenate(
            [dgain_s[kind], jnp.zeros((padded - rows - 1, width), F32)], axis=0
        )
        for at in range(0, CHIPS, 4):
            four = nn_dot(mt_s[kind, at * rows : (at + 4) * rows, :], cot_all)
            for i in range(4):
                store(at + i, jnp.concatenate([four[i * rows : (i + 1) * rows], below], axis=0))

    def store_given(chip, value):
        give_o[chip] = value.astype(BF16)

    o_rows(1 - core, store_given)
    for j in (3, 2, 1, 0):
        scatter_o.give(j)
    gather_o.finish()

    def keep_own(chip, value):
        wp[core, chip] = value.astype(BF16)

    o_rows(core, keep_own)

    def take_o(j):
        scatter_o.take(j, lambda n, chip: wp[core, chip].astype(F32))

    take_o(3)
    take_o(2)
    scatter_o.take_lent(3)
    scatter_o.send_far()
    take_o(1)
    take_o(0)
    scatter_q.take_lent(0)
    scatter_q.first_far()
    scatter_o.take_lent(2)
    scatter_o.send_near(2)
    scatter_o.take_lent(1)
    scatter_o.send_near(1)
    scatter_q.first_near()
    scatter_o.take_lent(0)
    for r in range(blocks):
        y, dx = y_s[0], dx_s[0]
        for b in range(1, blocks):
            y = jnp.where(rank_ref[b] == r, y_s[b], y)
            dx = jnp.where(rank_ref[b] == r, dx_s[b], dx)
        enc_ref[r] = y
        grad_ref[r] = dx
    scatter_o.first_far()
    scatter_q.swap(lambda value: (value[: share // 2], value[share // 2 :]))
    scatter_o.first_near()
    scatter_q.cross()

    def split_o(value):
        half = rows // 2
        below = jnp.concatenate([value[rows : rows + 1], jnp.zeros((3, width), F32)], axis=0)
        return (
            jnp.concatenate([value[:half], below], axis=0),
            jnp.concatenate([value[half:rows], below], axis=0),
        )

    scatter_o.swap(split_o)
    scatter_q.pair_up(out_q)
    scatter_o.cross()
    scatter_o.pair_up(out_o)
    scatter_q.end(out_q)
    scatter_o.end(out_o)
    for one in (early, gather_o, gather_q, scatter_q, scatter_o):
        one.finish()


def layer(kind, rank, blocks, cotangent, qkv_weight, out_weight, gain_row):
    count, window, width = blocks.shape
    inner = qkv_weight.shape[2] // 3
    tokens = count * window
    rows = inner // CHIPS
    padded = -(-(rows + 1) // 16) * 16
    q, o = (width // CHIPS, 3 * inner), (padded, width)
    half_q, half_o = qkv_weight.shape[1:], (-(-(rows // 2 + 1) // 8) * 8, width)
    scratch = [
        pltpu.VMEM((2, CHIPS) + q, BF16),
        pltpu.VMEM((2, CHIPS) + o, BF16),
        pltpu.VMEM((2, inner, width), BF16),
        pltpu.VMEM((2, 1, width), F32),
        pltpu.VMEM(qkv_weight.shape[1:], BF16),
        pltpu.VMEM(out_weight.shape[1:], BF16),
        pltpu.VMEM((1, width), F32),
        pltpu.VMEM((count, window, width), F32),
        pltpu.VMEM((count, window, LANES), F32),
        pltpu.VMEM((window, 3 * inner), BF16),
        pltpu.VMEM((window, inner), BF16),
        pltpu.VMEM((count, window, inner), BF16),
        pltpu.VMEM((count, window, 3 * inner), BF16),
        pltpu.VMEM((2, width, tokens), BF16),
        pltpu.VMEM((2, inner, tokens), BF16),
        pltpu.VMEM((count, window, width), BF16),
        pltpu.VMEM((count, window, width), BF16),
        pltpu.VMEM((2, 1, width), F32),
        pltpu.VMEM((CHIPS,) + q, BF16),
        pltpu.VMEM((CHIPS,) + o, BF16),
        pltpu.VMEM((CHIPS,) + q, BF16),
        pltpu.VMEM((CHIPS,) + o, BF16),
    ]
    for lead in ((4,), (4, 2), (), (2,)):
        scratch += [
            pltpu.VMEM(lead + (q[0], q[1] - AWAY_Q), BF16),
            pltpu.VMEM(lead + (o[0], o[1] - AWAY_O), BF16),
        ]
    scratch += [
        pltpu.VMEM((CHIPS, q[0], AWAY_Q), BF16),
        pltpu.VMEM((CHIPS, o[0], AWAY_O), BF16),
    ]
    for lead in ((2,), (), (3,)):
        scratch += [pltpu.VMEM(lead + half_q, BF16), pltpu.VMEM(lead + half_o, BF16)]
    scratch += [pltpu.SemaphoreType.DMA((2 * 48 + 3,))] * 2
    scratch += [pltpu.SemaphoreType.DMA((2 * STEPS,))] * 2
    vmem = pl.BlockSpec(memory_space=pltpu.VMEM)
    return pl.pallas_call(
        layer_kernel,
        out_shape=(
            jax.ShapeDtypeStruct(blocks.shape, BF16),
            jax.ShapeDtypeStruct(blocks.shape, BF16),
            jax.ShapeDtypeStruct(half_q, F32),
            jax.ShapeDtypeStruct(half_o, F32),
        ),
        in_specs=[pl.BlockSpec(memory_space=pltpu.SMEM)] * 2 + [vmem] * 5,
        out_specs=(vmem,) * 4,
        scratch_shapes=scratch,
        compiler_params=pltpu.CompilerParams(
            collective_id=0, has_side_effects=True, vmem_limit_bytes=VMEM_BYTES
        ),
    )(kind, rank, blocks, cotangent, qkv_weight, out_weight, gain_row)


def shards(blocks, cotangent, modality, time_rank, qkv_weight, out_weight, norm_gain):
    rows, width = out_weight.shape[1:]
    share = norm_gain.shape[1]
    start = lax.axis_index("dp") * share
    gain_row = lax.dynamic_update_slice(
        jnp.zeros((2, width), F32), norm_gain.astype(F32), (0, start)
    )[:, None, :]
    encoded, block_grad, share_qkv, share_packed = layer(
        modality, time_rank, blocks, cotangent, qkv_weight, out_weight, gain_row
    )
    share_gain = lax.dynamic_slice(share_packed, (rows, start), (1, share))
    return (encoded, block_grad, share_qkv[None], share_packed[None, :rows], share_gain)


def solution(mesh):
    return jax.shard_map(
        shards,
        mesh=mesh,
        in_specs=(
            P(("grp", "dp"), None, None),
            P(("grp", "dp"), None, None),
            P(("grp", "dp")),
            P(("grp", "dp")),
            P(None, "dp", None),
            P(None, "dp", None),
            P(None, "dp"),
        ),
        out_specs=(
            P(("grp", "dp"), None, None),
            P(("grp", "dp"), None, None),
            P("grp", "dp", None),
            P("grp", "dp", None),
            P("grp", "dp"),
        ),
        check_vma=False,
    )
```

```python
import math

import jax
import jax.numpy as jnp
from jax import lax
from jax.experimental import pallas as pl
from jax.experimental.pallas import tpu as pltpu
from jax.sharding import PartitionSpec as P

A_HEADS = 10
A_SIZE = 64
V_HEADS = 8
V_SIZE = 80
WIN = 128
VWIN = 64
LANES = 128
EPSILON = 1e-05
VMEM_BYTES = 62 * 1024 * 1024
RING = 4
CHIPS = RING * RING
STEPS = 51
BEHIND = 6
AWAY_Q, AWAY_O = 5 * LANES, 3 * LANES
MESH = pl.DeviceIdType.MESH
OFFSETS = (0, -1, 1, 2)
UP = (True, False, False, True)
BF16, F32 = jnp.bfloat16, jnp.float32


def normalized(x):
    mean_row = jnp.mean(x, axis=-1, keepdims=True)
    centered = x - mean_row
    inverse = lax.rsqrt(jnp.mean(centered * centered, axis=-1, keepdims=True) + EPSILON)
    return centered * inverse, inverse


def nt_dot(a, b):
    return lax.dot_general(a, b, (((1,), (1,)), ((), ())), preferred_element_type=F32)


def tn_dot(a, b):
    return lax.dot_general(a, b, (((0,), (0,)), ((), ())), preferred_element_type=F32)


def nn_dot(a, b):
    return jnp.dot(a, b, preferred_element_type=F32)


def attend_pair(query, keys, values, cot, first, second, scale, same_window):
    zero = jnp.zeros((), BF16)

    def stacked(rows):
        return jnp.concatenate(
            [jnp.where(first, rows, zero), jnp.where(second, rows, zero)], axis=0
        )

    query_two = stacked(query)
    cot_two = stacked(cot)
    scores = jnp.where(same_window, nt_dot(query_two, keys) * scale, -1e30)
    row_max = jnp.max(scores, axis=-1, keepdims=True)
    exponent = jnp.exp(scores - row_max)
    probs = exponent * (1.0 / jnp.sum(exponent, axis=-1, keepdims=True))
    probs_low = probs.astype(BF16)
    d_probs = nt_dot(cot_two, values)
    inner = jnp.sum(d_probs * probs, axis=-1, keepdims=True)
    d_scores = (probs * (d_probs - inner) * scale).astype(BF16)

    def beside(rows):
        return jnp.concatenate([rows[:WIN], rows[WIN:]], axis=1)

    mixed = nn_dot(beside(probs_low), stacked(values))
    d_values = tn_dot(probs_low, cot_two)
    d_query = nn_dot(beside(d_scores), stacked(keys))
    d_keys = tn_dot(d_scores, query_two)
    return mixed, d_query, d_keys, d_values


def attend_block(audio, qkv, cot, out, d_qkv):
    inner = cot.shape[1]
    tile_count = inner // LANES
    scale = jnp.where(audio, 1.0 / math.sqrt(A_SIZE), 1.0 / math.sqrt(V_SIZE)).astype(F32)
    size = jnp.where(audio, A_SIZE, V_SIZE)
    row = lax.broadcasted_iota(jnp.int32, (2 * WIN, WIN), 0)
    col = lax.broadcasted_iota(jnp.int32, (2 * WIN, WIN), 1)
    apart = ((row % WIN) // VWIN != col // VWIN).astype(jnp.int32)
    same_window = apart * jnp.where(audio, 0, 1) == 0
    tiles = [[None] * tile_count for _ in range(4)]
    for pair in range(A_HEADS // 2):
        start, stop = pair * LANES, min((pair + 2) * LANES, inner)
        low = jnp.where(audio, 2 * pair * A_SIZE, 2 * pair * V_SIZE)
        lane = lax.broadcasted_iota(jnp.int32, (WIN, stop - start), 1) + start
        first = (lane >= low) & (lane < low + size)
        second = (lane >= low + size) & (lane < low + 2 * size)
        found = attend_pair(
            qkv[:, start:stop],
            qkv[:, inner + start : inner + stop],
            qkv[:, 2 * inner + start : 2 * inner + stop],
            cot[:, start:stop],
            first,
            second,
            scale,
            same_window,
        )
        for which in range(4):
            for tile in range(start // LANES, stop // LANES):
                at = tile * LANES - start
                part = found[which][:, at : at + LANES]
                held = tiles[which][tile]
                tiles[which][tile] = part if held is None else held + part
        at = slice(start, start + LANES)
        out[:, at] = tiles[0][pair].astype(BF16)
        for which in range(3):
            to = slice(which * inner + start, which * inner + start + LANES)
            d_qkv[:, to] = tiles[which + 1][pair].astype(BF16)


def step_on(position, by):
    return lax.rem(position + by + RING, RING)


class Torus:
    def __init__(self):
        self.row = lax.axis_index("grp")
        self.index = lax.axis_index("dp")
        self.core = self.index % 2
        self.y, self.z = self.index // (2 * RING), self.index // 2 % RING

    def chip(self, first_by, second_by, kind):
        y_by = jnp.where(kind == 0, first_by, second_by)
        z_by = jnp.where(kind == 0, second_by, first_by)
        return step_on(self.y, y_by) * RING + step_on(self.z, z_by)

    def near(self, first_by, second_by):
        return (self.row, self.chip(first_by, second_by, self.core) * 2 + self.core)

    def meet(self):
        self.sibling = (self.row, self.index + 1 - 2 * self.core)
        self.across = (RING - 1 - self.row, self.index)
        self.beside = (self.row + 1 - 2 * (self.row % 2), self.index)
        peers = [self.near(1, 0), self.near(-1, 0), self.near(0, 1), self.near(0, -1)]
        peers += [self.sibling, self.across, self.beside]
        barrier = pltpu.get_barrier_semaphore()
        for peer in peers:
            pl.semaphore_signal(barrier, inc=1, device_id=peer, device_id_type=MESH)
        pl.semaphore_wait(barrier, len(peers))


class Lane:
    def __init__(self, base, send_sem, recv_sem, sibling):
        self.base, self.send_sem, self.recv_sem = base, send_sem, recv_sem
        self.sibling = sibling
        self.sent = []

    def copy(self, number, source, target, device):
        return pltpu.make_async_remote_copy(
            src_ref=source,
            dst_ref=target,
            send_sem=self.send_sem.at[self.base + number],
            recv_sem=self.recv_sem.at[self.base + number],
            device_id=device,
            device_id_type=MESH,
        )

    def send(self, number, source, target, device):
        made = self.copy(number, source, target, device)
        made.start()
        self.sent.append(made)

    def arrive(self, number, target):
        self.copy(number, target, target, self.sibling).wait_recv()

    def finish(self):
        for made in self.sent:
            made.wait_send()
        self.sent = []


class Slots(Lane):
    def __init__(self, base, send_sem, recv_sem, torus, columns, away):
        super().__init__(base, send_sem, recv_sem, torus.sibling)
        self.torus, self.away, self.carried = torus, away, columns - away
        odd = torus.row % 2
        self.start = pl.multiple_of(away * (1 - odd), LANES)
        self.missing = pl.ds(pl.multiple_of(self.carried * odd, LANES), away)
        self.lent = pl.ds(pl.multiple_of(self.carried * (1 - odd), LANES), away)
        self.cut = -(-self.carried // (2 * LANES)) * LANES

    def chip(self, n, j):
        return self.torus.chip(OFFSETS[n], OFFSETS[j], self.torus.core)

    def window(self):
        return pl.ds(self.start, self.carried)

    def half_window(self, upper):
        if upper:
            return pl.ds(self.start + self.cut, self.carried - self.cut)
        return pl.ds(self.start, self.cut)

    def neighbour(self, n, j):
        return self.torus.across if (n + j) % 2 else self.torus.beside


class Gather(Slots):
    def __init__(self, base, send_sem, recv_sem, torus, held, away, pending):
        super().__init__(base, send_sem, recv_sem, torus, held.shape[-1], away)
        self.held, self.pending = held, pending

    def slot(self, n, j, columns=None):
        columns = self.window() if columns is None else columns
        return self.held.at[self.torus.core, self.chip(n, j), :, columns]

    def half(self, n, upper):
        return self.slot(n, 0, self.half_window(upper))

    def pass_on(self, number, view, first_by, second_by):
        self.send(number, view, view, self.torus.near(first_by, second_by))

    def share(self, n, j):
        view = self.held.at[self.torus.core, self.chip(n, j)]
        self.send(16 + 4 * n + j, view, view, self.sibling)

    def lend(self, n, j):
        view = self.slot(n, j, self.lent)
        self.send(32 + 4 * n + j, view, view, self.neighbour(n, j))
        self.pending.append((self, n, j))
        if len(self.pending) > BEHIND:
            one, n, j = self.pending.pop(0)
            one.complete(n, j)

    def complete(self, n, j):
        self.arrive(32 + 4 * n + j, self.slot(n, j, self.missing))
        self.share(n, j)

    def along_second(self, n):
        self.pass_on(4 + 2 * n, self.slot(n, 0), 0, 1)
        self.pass_on(5 + 2 * n, self.slot(n, 0), 0, -1)

    def begin(self):
        self.pass_on(0, self.slot(0, 0), 1, 0)
        self.pass_on(1, self.slot(0, 0), -1, 0)
        self.along_second(0)
        self.share(0, 0)

    def ring_back(self):
        self.arrive(0, self.slot(1, 0))
        self.pass_on(2, self.half(1, False), 1, 0)
        self.along_second(1)
        self.lend(1, 0)

    def ring_ahead(self):
        self.arrive(1, self.slot(2, 0))
        self.pass_on(3, self.half(2, True), -1, 0)
        self.along_second(2)
        self.lend(2, 0)

    def ring_far(self):
        self.arrive(2, self.half(3, False))
        self.arrive(3, self.half(3, True))
        self.along_second(3)
        self.lend(3, 0)

    def second_near(self, n):
        self.arrive(4 + 2 * n, self.slot(n, 1))
        if UP[n]:
            self.pass_on(12 + n, self.slot(n, 1), 0, 1)
        self.lend(n, 1)
        self.arrive(5 + 2 * n, self.slot(n, 2))
        if not UP[n]:
            self.pass_on(12 + n, self.slot(n, 2), 0, -1)
        self.lend(n, 2)

    def second_far(self, n):
        self.arrive(12 + n, self.slot(n, 3))
        self.lend(n, 3)

    def other_kind(self):
        other = 1 - self.torus.core
        for j in range(4):
            for n in range(4):
                chip = self.torus.chip(OFFSETS[n], OFFSETS[j], other)
                self.arrive(16 + 4 * n + j, self.held.at[other, chip])


class Scatter(Slots):
    def __init__(self, base, send_sem, recv_sem, torus, given, total, held, away):
        super().__init__(base, send_sem, recv_sem, torus, total.shape[-1], away)
        self.given, self.total = given, total
        self.one, self.two, self.three, self.four, self.lent_in = held[:5]
        self.kinds, self.leave, self.row_in = held[5:]

    def view(self, n, j, columns=None):
        columns = self.window() if columns is None else columns
        return self.total.at[self.chip(n, j), :, columns]

    def part(self, upper):
        return self.three.at[:, slice(self.cut, None) if upper else slice(0, self.cut)]

    def add(self, target, *terms):
        value = target[...].astype(F32)
        for term in terms:
            value = value + term[...].astype(F32)
        target[...] = value.astype(BF16)

    def give(self, j):
        for n in range(4):
            chip = self.torus.chip(OFFSETS[n], OFFSETS[j], 1 - self.torus.core)
            self.send(4 * j + n, self.given.at[chip], self.total.at[chip], self.sibling)

    def take(self, j, own):
        for n in range(4):
            chip = self.chip(n, j)
            self.arrive(4 * j + n, self.total.at[chip])
            value = own(n, chip) + self.total[chip].astype(F32)
            self.total[chip] = value.astype(BF16)
            if n or j:
                lent = self.view(n, j, self.missing)
                self.send(32 + 4 * j + n, lent, self.lent_in.at[4 * j + n], self.neighbour(n, j))

    def take_lent(self, j):
        for n in range(4):
            if n or j:
                self.arrive(32 + 4 * j + n, self.lent_in.at[4 * j + n])
                self.add(self.view(n, j, self.lent), self.lent_in.at[4 * j + n])

    def send_far(self):
        for n in range(4):
            device = self.torus.near(0, 1 if UP[n] else -1)
            self.send(16 + n, self.view(n, 3), self.one.at[n], device)

    def send_near(self, j):
        for n in (3, 1, 2, 0):
            if UP[n] == (j == 2):
                self.arrive(16 + n, self.one.at[n])
                self.add(self.view(n, j), self.one.at[n])
            number, which = (20 + 2 * n, 0) if j == 2 else (21 + 2 * n, 1)
            device = self.torus.near(0, OFFSETS[j])
            self.send(number, self.view(n, j), self.two.at[n, which], device)

    def close_second(self, n):
        self.arrive(20 + 2 * n, self.two.at[n, 0])
        self.arrive(21 + 2 * n, self.two.at[n, 1])
        self.add(self.view(n, 0), self.two.at[n, 0], self.two.at[n, 1])

    def first_far(self):
        self.close_second(3)
        for upper, by in ((False, 1), (True, -1)):
            view = self.view(3, 0, self.half_window(upper))
            self.send(28 + upper, view, self.part(upper), self.torus.near(by, 0))
        for n in (2, 1, 0):
            self.close_second(n)

    def first_near(self):
        for n, upper, by in ((2, False, 1), (1, True, -1)):
            self.arrive(28 + upper, self.part(upper))
            self.add(self.view(n, 0, self.half_window(upper)), self.part(upper))
            self.send(30 + upper, self.view(n, 0), self.four.at[int(upper)], self.torus.near(by, 0))

    def swap(self, split):
        self.arrive(30, self.four.at[0])
        self.arrive(31, self.four.at[1])
        self.add(self.view(0, 0), self.four.at[0], self.four.at[1])
        low, high = split(self.total[self.chip(0, 0)].astype(F32))
        core = self.torus.core
        self.kinds[core] = jnp.where(core == 0, low, high).astype(BF16)
        self.leave[...] = jnp.where(core == 0, high, low).astype(BF16)
        self.send(48, self.leave, self.kinds.at[core], self.sibling)

    def cross(self):
        kind = self.torus.row // 2
        self.arrive(48, self.kinds.at[1 - self.torus.core])
        self.send(49, self.kinds.at[1 - kind], self.row_in.at[0], self.torus.across)

    def pair_up(self, out):
        kind = self.torus.row // 2
        self.arrive(49, self.row_in.at[0])
        value = self.kinds[kind].astype(F32) + self.row_in[0].astype(F32)
        out[...] = value
        self.row_in[1] = value.astype(BF16)
        self.send(50, self.row_in.at[1], self.row_in.at[2], self.torus.beside)

    def end(self, out):
        self.arrive(50, self.row_in.at[2])
        out[...] += self.row_in[2].astype(F32)


def layer_kernel(
    kind_ref, rank_ref, x_ref, cot_ref, q_in, o_in, gain_in,
    enc_ref, grad_ref, out_q, out_o,
    wq, wp, wo, gain_s, sib_q, sib_o, sib_gain, xhat_s, inv_s, qkv_s, dattn_s, mixed_s, dqkv_s, ht_s, mt_s,
    y_s, dx_s, enc_s, grad_s, out_sem, dgain_s, give_q, give_o, total_q, total_o, *rest,
):
    held_q, held_o = rest[0:16:2], rest[1:16:2]
    gather_send, gather_recv, scatter_send, scatter_recv = rest[16:]
    blocks, window, width = x_ref.shape
    inner = wo.shape[1]
    rows = inner // CHIPS
    share = width // CHIPS
    padded = wp.shape[2]
    torus = Torus()
    torus.meet()
    core = torus.core
    first = core == 0

    early = Lane(2 * 48, gather_send, gather_recv, torus.sibling)
    early.send(0, o_in.at[1 - core], sib_o, torus.sibling)
    early.send(1, gain_in.at[1 - core], sib_gain, torus.sibling)
    early.send(2, q_in.at[1 - core], sib_q, torus.sibling)
    pending = []
    gather_o = Gather(0, gather_send, gather_recv, torus, wp, AWAY_O, pending)
    gather_q = Gather(48, gather_send, gather_recv, torus, wq, AWAY_Q, pending)
    gathers = (gather_o, gather_q)
    here = torus.y * RING + torus.z
    early.arrive(0, sib_o)
    early.arrive(1, sib_gain)
    mine, other = o_in[core].astype(F32), sib_o[...].astype(F32)
    gain_row = gain_in[core] + sib_gain[...]
    wp[core, here] = jnp.concatenate(
        [
            jnp.where(first, mine, other),
            jnp.where(first, other, mine),
            gain_row,
            jnp.zeros((padded - 2 * mine.shape[0] - 1, width), F32),
        ],
        axis=0,
    ).astype(BF16)
    gather_o.begin()
    early.arrive(2, sib_q)
    mine, other = q_in[core].astype(F32), sib_q[...].astype(F32)
    wq[core, here] = jnp.concatenate(
        [jnp.where(first, mine, other), jnp.where(first, other, mine)], axis=0
    ).astype(BF16)
    gather_q.begin()

    def norm_block(b):
        x_hat, inverse = normalized(x_ref[b].astype(F32))
        xhat_s[b] = x_hat
        inv_s[b] = jnp.broadcast_to(inverse, inv_s.shape[1:])

    norm_block(0)
    for one in gathers:
        one.ring_back()
        one.ring_ahead()
    norm_block(1)
    for one in gathers:
        one.second_near(0)
    norm_block(2)
    for one in gathers:
        one.ring_far()
    norm_block(3)
    for one in gathers:
        one.second_near(1)
        one.second_near(2)
        one.second_far(0)
    for one in gathers:
        one.second_near(3)
        one.second_far(1)
        one.second_far(2)
        one.second_far(3)
    for one, n, j in pending:
        one.complete(n, j)
    gather_o.other_kind()

    @pl.loop(0, 2)
    def _(m):
        for chip in range(0, CHIPS, 2):
            two = [wp[m, chip + i, 0:rows].astype(F32) for i in range(2)]
            wo[m, chip * rows : (chip + 2) * rows] = jnp.concatenate(two, axis=0).astype(BF16)
        gain_s[m] = sum(wp[m, chip, rows : rows + 1].astype(F32) for chip in range(CHIPS))

    gather_q.other_kind()

    def weights(kind, low, high):
        return wq[kind, :, :, low:high].reshape(width, high - low)

    @pl.loop(0, blocks)
    def _(b):
        kind = kind_ref[b]
        normed = (xhat_s[b] * gain_s[kind]).astype(BF16)
        columns = pl.ds(pl.multiple_of(b * WIN, WIN), WIN)
        turned = normed.T
        for m in range(2):
            ht_s[m, :, columns] = jnp.where(kind == m, turned, jnp.zeros_like(turned))
        for at in range(0, 3 * inner, inner):
            qkv_s[:, at : at + inner] = nn_dot(normed, weights(kind, at, at + inner)).astype(BF16)
        dattn_s[...] = nt_dot(cot_ref[b], wo[kind]).astype(BF16)
        attend_block(kind == 0, qkv_s, dattn_s, mixed_s.at[b], dqkv_s.at[b])
        mixed_t = mixed_s[b].T
        for m in range(2):
            mt_s[m, :, columns] = jnp.where(kind == m, mixed_t, jnp.zeros_like(mixed_t))

    scatter_q = Scatter(
        0, scatter_send, scatter_recv, torus, give_q, total_q, held_q, AWAY_Q
    )
    scatter_o = Scatter(
        STEPS, scatter_send, scatter_recv, torus, give_o, total_o, held_o, AWAY_O
    )
    tokens = blocks * window
    d_qkv_all = dqkv_s[...].reshape(tokens, 3 * inner)

    def q_block(kind, j):
        parts = []
        for n in range(4):
            chip = torus.chip(OFFSETS[n], OFFSETS[j], kind)
            at = pl.ds(pl.multiple_of(chip * share, 16), share)
            parts.append(ht_s[kind, at, :])
        return nn_dot(jnp.concatenate(parts, axis=0), d_qkv_all)

    for j in (3, 2, 1, 0):
        found = q_block(1 - core, j)
        for n in range(4):
            chip = torus.chip(OFFSETS[n], OFFSETS[j], 1 - core)
            give_q[chip] = found[n * share : (n + 1) * share].astype(BF16)
        scatter_q.give(j)

    def take_q(j):
        found = q_block(core, j)
        scatter_q.take(j, lambda n, chip: found[n * share : (n + 1) * share])

    take_q(3)
    take_q(2)
    scatter_q.take_lent(3)
    scatter_q.send_far()
    take_q(1)
    scatter_q.take_lent(2)
    scatter_q.send_near(2)
    scatter_q.take_lent(1)
    scatter_q.send_near(1)
    take_q(0)
    dgain_s[...] = jnp.zeros_like(dgain_s)

    def finish_blocks(low, high):
        @pl.loop(low, high)
        def _(b):
            kind = kind_ref[b]
            x_hat = xhat_s[b]
            gain = gain_s[kind]
            y = x_ref[b].astype(F32) + nn_dot(mixed_s[b], wo[kind])
            y_s[b] = y.astype(BF16)
            d_normed = nt_dot(dqkv_s[b], weights(kind, 0, 3 * inner))
            d_gain = jnp.sum(d_normed * x_hat, axis=0, keepdims=True)
            for m in range(2):
                dgain_s[m] += jnp.where(kind == m, d_gain, jnp.zeros_like(d_gain))
            scaled = d_normed * gain
            d_input = inv_s[b][:, 0:1] * (
                scaled
                - jnp.mean(scaled, axis=-1, keepdims=True)
                - x_hat * jnp.mean(scaled * x_hat, axis=-1, keepdims=True)
            )
            dx_s[b] = (cot_ref[b].astype(F32) + d_input).astype(BF16)

    finish_blocks(0, blocks)
    cot_all = cot_ref[...].reshape(tokens, width)

    def o_rows(kind, store):
        below = jnp.concatenate(
            [dgain_s[kind], jnp.zeros((padded - rows - 1, width), F32)], axis=0
        )
        for at in range(0, CHIPS, 4):
            four = nn_dot(mt_s[kind, at * rows : (at + 4) * rows, :], cot_all)
            for i in range(4):
                store(at + i, jnp.concatenate([four[i * rows : (i + 1) * rows], below], axis=0))

    def store_given(chip, value):
        give_o[chip] = value.astype(BF16)

    o_rows(1 - core, store_given)
    for j in (3, 2, 1, 0):
        scatter_o.give(j)
    gather_o.finish()

    def keep_own(chip, value):
        wp[core, chip] = value.astype(BF16)

    o_rows(core, keep_own)

    def take_o(j):
        scatter_o.take(j, lambda n, chip: wp[core, chip].astype(F32))

    take_o(3)
    take_o(2)
    scatter_o.take_lent(3)
    scatter_o.send_far()
    take_o(1)
    take_o(0)
    scatter_q.take_lent(0)
    scatter_q.first_far()
    scatter_o.take_lent(2)
    scatter_o.send_near(2)
    scatter_o.take_lent(1)
    scatter_o.send_near(1)
    scatter_q.first_near()
    scatter_o.take_lent(0)
    leaving = []
    for r in range(blocks):
        y, dx = y_s[0], dx_s[0]
        for b in range(1, blocks):
            y = jnp.where(rank_ref[b] == r, y_s[b], y)
            dx = jnp.where(rank_ref[b] == r, dx_s[b], dx)
        enc_s[r] = y
        grad_s[r] = dx
        for number, (held, ref) in enumerate(((enc_s, enc_ref), (grad_s, grad_ref))):
            leaving.append(pltpu.make_async_copy(held.at[r], ref.at[r], out_sem.at[2 * r + number]))
            leaving[-1].start()
    scatter_o.first_far()
    scatter_q.swap(lambda value: (value[: share // 2], value[share // 2 :]))
    scatter_o.first_near()
    scatter_q.cross()

    def split_o(value):
        half = rows // 2
        below = jnp.concatenate([value[rows : rows + 1], jnp.zeros((3, width), F32)], axis=0)
        return (
            jnp.concatenate([value[:half], below], axis=0),
            jnp.concatenate([value[half:rows], below], axis=0),
        )

    scatter_o.swap(split_o)
    scatter_q.pair_up(out_q)
    scatter_o.cross()
    scatter_o.pair_up(out_o)
    scatter_q.end(out_q)
    scatter_o.end(out_o)
    for made in leaving:
        made.wait()
    for one in (early, gather_o, gather_q, scatter_q, scatter_o):
        one.finish()


def layer(kind, rank, blocks, cotangent, qkv_weight, out_weight, gain_row):
    count, window, width = blocks.shape
    inner = qkv_weight.shape[2] // 3
    tokens = count * window
    rows = inner // CHIPS
    padded = -(-(rows + 1) // 16) * 16
    q, o = (width // CHIPS, 3 * inner), (padded, width)
    half_q, half_o = qkv_weight.shape[1:], (-(-(rows // 2 + 1) // 8) * 8, width)
    scratch = [
        pltpu.VMEM((2, CHIPS) + q, BF16),
        pltpu.VMEM((2, CHIPS) + o, BF16),
        pltpu.VMEM((2, inner, width), BF16),
        pltpu.VMEM((2, 1, width), F32),
        pltpu.VMEM(qkv_weight.shape[1:], BF16),
        pltpu.VMEM(out_weight.shape[1:], BF16),
        pltpu.VMEM((1, width), F32),
        pltpu.VMEM((count, window, width), F32),
        pltpu.VMEM((count, window, LANES), F32),
        pltpu.VMEM((window, 3 * inner), BF16),
        pltpu.VMEM((window, inner), BF16),
        pltpu.VMEM((count, window, inner), BF16),
        pltpu.VMEM((count, window, 3 * inner), BF16),
        pltpu.VMEM((2, width, tokens), BF16),
        pltpu.VMEM((2, inner, tokens), BF16),
        pltpu.VMEM((count, window, width), BF16),
        pltpu.VMEM((count, window, width), BF16),
        pltpu.VMEM((count, window, width), BF16),
        pltpu.VMEM((count, window, width), BF16),
        pltpu.SemaphoreType.DMA((2 * count,)),
        pltpu.VMEM((2, 1, width), F32),
        pltpu.VMEM((CHIPS,) + q, BF16),
        pltpu.VMEM((CHIPS,) + o, BF16),
        pltpu.VMEM((CHIPS,) + q, BF16),
        pltpu.VMEM((CHIPS,) + o, BF16),
    ]
    for lead in ((4,), (4, 2), (), (2,)):
        scratch += [
            pltpu.VMEM(lead + (q[0], q[1] - AWAY_Q), BF16),
            pltpu.VMEM(lead + (o[0], o[1] - AWAY_O), BF16),
        ]
    scratch += [
        pltpu.VMEM((CHIPS, q[0], AWAY_Q), BF16),
        pltpu.VMEM((CHIPS, o[0], AWAY_O), BF16),
    ]
    for lead in ((2,), (), (3,)):
        scratch += [pltpu.VMEM(lead + half_q, BF16), pltpu.VMEM(lead + half_o, BF16)]
    scratch += [pltpu.SemaphoreType.DMA((2 * 48 + 3,))] * 2
    scratch += [pltpu.SemaphoreType.DMA((2 * STEPS,))] * 2
    vmem = pl.BlockSpec(memory_space=pltpu.VMEM)
    return pl.pallas_call(
        layer_kernel,
        out_shape=(
            jax.ShapeDtypeStruct(blocks.shape, BF16),
            jax.ShapeDtypeStruct(blocks.shape, BF16),
            jax.ShapeDtypeStruct(half_q, F32),
            jax.ShapeDtypeStruct(half_o, F32),
        ),
        in_specs=[pl.BlockSpec(memory_space=pltpu.SMEM)] * 2 + [vmem] * 5,
        out_specs=(pl.BlockSpec(memory_space=pl.ANY),) * 2 + (vmem,) * 2,
        scratch_shapes=scratch,
        compiler_params=pltpu.CompilerParams(
            collective_id=0, has_side_effects=True, vmem_limit_bytes=VMEM_BYTES
        ),
    )(kind, rank, blocks, cotangent, qkv_weight, out_weight, gain_row)


def shards(blocks, cotangent, modality, time_rank, qkv_weight, out_weight, norm_gain):
    rows, width = out_weight.shape[1:]
    share = norm_gain.shape[1]
    start = lax.axis_index("dp") * share
    gain_row = lax.dynamic_update_slice(
        jnp.zeros((2, width), F32), norm_gain.astype(F32), (0, start)
    )[:, None, :]
    encoded, block_grad, share_qkv, share_packed = layer(
        modality, time_rank, blocks, cotangent, qkv_weight, out_weight, gain_row
    )
    share_gain = lax.dynamic_slice(share_packed, (rows, start), (1, share))
    return (encoded, block_grad, share_qkv[None], share_packed[None, :rows], share_gain)


def solution(mesh):
    return jax.shard_map(
        shards,
        mesh=mesh,
        in_specs=(
            P(("grp", "dp"), None, None),
            P(("grp", "dp"), None, None),
            P(("grp", "dp")),
            P(("grp", "dp")),
            P(None, "dp", None),
            P(None, "dp", None),
            P(None, "dp"),
        ),
        out_specs=(
            P(("grp", "dp"), None, None),
            P(("grp", "dp"), None, None),
            P("grp", "dp", None),
            P("grp", "dp", None),
            P("grp", "dp"),
        ),
        check_vma=False,
    )
```
